256 devices in a mesh: row: 8 (over y, core), col: 32 (over z, x).
Axes of the slice: x: 4, y: 4, z: 8, core: 2. Of those that a mesh axis runs over, the one named last changes fastest.
Arguments:
- user_factors: bfloat16 [32768, 64], P(('row', 'col')), may hold values from -4 to 4
- item_factors: bfloat16 [65536, 64], P(('col', 'row')), may hold values from -4 to 4
- start_vectors: bfloat16 [65536, 128], P(('col', 'row')), may hold values from -6 to 6
- ratings: bfloat16 [8, 32, 96, 128, 128], P('row', 'col'), may hold values from -6 to 6
- tile_rows: int32 [8, 32, 96], P('row', 'col'), may hold values from 0 to 31, as said below
- tile_cols: int32 [8, 32, 96], P('row', 'col'), may hold values from 0 to 15, as said below
- tile_count: int32 [8, 32], P('row', 'col'), may hold values from 32 to 96, as said below
Outputs:
- user_basis_out: float32 [32768, 128], P(('row', 'col'))
- item_basis_out: float32 [65536, 128], P(('col', 'row'))
The draws below stay inside these ranges and needn't reach their ends.
Inputs may be any that keep to these rules, and one draw needn't show every extreme that they name: `tile_rows`: within one device the slots name distinct tiles of its blocks. `tile_cols`: within one device the slots name distinct tiles of its blocks. `tile_count`: some device uses all 96 slots in every draw; slots at or past a device's count are unused.
All inputs are finite; a program needn't handle non-finite values.
Results may differ from the reference program's by a relative error of at most 0.009.
Values may be sent and summed in bfloat16 or wider, within the bound.
No kernel may reach another device: no remote copies, remote signals or barrier semaphores. Data moves between devices by JAX's collectives and lax.ppermute only.
A program may use at most 64 MiB of HBM per device.

```python
import jax
import jax.numpy as jnp
from jax import lax

TILE = 128
R = 64
VECS = 128
TU = 32
TI = 16
K = 96
USERS = 32768
ITEMS = 65536
N_ROW = 8
N_COL = 32


def tile_pairs(key):
    keys = jax.random.split(key, N_ROW * N_COL)
    picks = jax.vmap(lambda single: jax.random.permutation(single, TU * TI)[:K])(keys)
    return picks.reshape(N_ROW, N_COL, K).astype(jnp.int32)


def draw_tile_rows(key, part):
    picks = tile_pairs(key)
    return (picks // TI).astype(jnp.int32)


def draw_tile_cols(key, part):
    picks = tile_pairs(key)
    return (picks % TI).astype(jnp.int32)


def draw_tile_count(key, part):
    key = jax.random.fold_in(key, 7)
    first, second = jax.random.split(key)
    counts = jax.random.randint(first, (N_ROW * N_COL,), K // 3, K + 1, dtype=jnp.int32)
    chosen = jax.random.randint(second, (), 0, N_ROW * N_COL, dtype=jnp.int32)
    counts = counts.at[chosen].set(K)
    return counts.reshape(N_ROW, N_COL).astype(jnp.int32)


def block_levels(stream_key, dims, cuts, smallest, largest):
    level = 1.0
    for dim, parts in cuts:
        draws = jax.random.uniform(jax.random.fold_in(jax.random.fold_in(stream_key, 6), dim), (parts,), jnp.float32, smallest / len(cuts), largest / len(cuts))
        level = level * jnp.repeat(jnp.exp(draws), dims[dim] // parts).reshape((-1,) + (1,) * (len(dims) - 1 - dim))
    return level


def gaussian(stream_key, extent, scale, limit, cuts=(), kind=jnp.bfloat16):
    array = scale * jax.random.normal(stream_key, extent, jnp.float32)
    if cuts:
        array = array * block_levels(stream_key, extent, cuts, -0.22, 0.18)
    return jnp.clip(array, -limit, limit).astype(kind)


def setup_inputs(seed: int = 0) -> dict:
    key_of = jax.random.split(jax.random.key(seed), 8)
    return {
        "user_factors": gaussian(key_of[0], (USERS, R), 0.25, 4.0, ((0, 256),)),
        "item_factors": gaussian(key_of[1], (ITEMS, R), 0.25, 4.0, ((0, 256),)),
        "start_vectors": gaussian(key_of[2], (ITEMS, VECS), 1.0, 6.0, ((0, 256),)),
        "ratings": gaussian(key_of[3], (N_ROW, N_COL, K, TILE, TILE), 1.0, 6.0, ((0, 8), (1, 32))),
        "tile_rows": draw_tile_rows(jax.random.fold_in(key_of[7], 71), 0),
        "tile_cols": draw_tile_cols(jax.random.fold_in(key_of[7], 71), 0),
        "tile_count": draw_tile_count(jax.random.fold_in(key_of[7], 71), 0),
    }


def device_residual(user_tiles, item_tiles, rating, rows, cols, valid):
    left = user_tiles[rows].astype(jnp.float32)
    right = item_tiles[cols].astype(jnp.float32)
    product = jnp.einsum('kir,kjr->kij', left, right)
    res = (product - rating.astype(jnp.float32)) * valid[:, None, None]
    return res.astype(jnp.bfloat16)

def orthonormal(block):
    gram = jnp.dot(block.T.astype(jnp.float32), block.astype(jnp.float32), precision=lax.Precision.HIGHEST, preferred_element_type=jnp.float32)
    lower = jnp.linalg.cholesky(gram)
    return lax.linalg.triangular_solve(lower, block, left_side=False, lower=True, transpose_a=True)

def reference(user_factors, item_factors, start_vectors, ratings, tile_rows, tile_cols, tile_count):
    user_tiles = user_factors.reshape(USERS // TILE, TILE, R)
    item_tiles = item_factors.reshape(ITEMS // TILE, TILE, R)
    slots = jnp.arange(K, dtype=jnp.int32)

    def device_data(index):
        rdev = index // N_COL
        cdev = index % N_COL
        rows = (tile_rows[rdev, cdev] + rdev * TU).astype(jnp.int32)
        cols = (tile_cols[rdev, cdev] + cdev * TI).astype(jnp.int32)
        valid = (slots < tile_count[rdev, cdev]).astype(jnp.float32)
        res = device_residual(user_tiles, item_tiles, ratings[rdev, cdev], rows, cols, valid)
        return (res, rows, cols)

    def forward(basis):
        basis_tiles = basis.reshape(ITEMS // TILE, TILE, VECS)

        def step(total, index):
            res, rows, cols = device_data(index)
            contrib = jnp.einsum('kij,kjc->kic', res.astype(jnp.float32), basis_tiles[cols].astype(jnp.float32))
            return (total.at[rows].add(contrib), None)
        start = jnp.zeros((USERS // TILE, TILE, VECS), jnp.float32)
        total, _ = lax.scan(step, start, jnp.arange(N_ROW * N_COL, dtype=jnp.int32))
        return total.reshape(USERS, VECS)

    def backward(basis):
        basis_tiles = basis.reshape(USERS // TILE, TILE, VECS)

        def step(total, index):
            res, rows, cols = device_data(index)
            contrib = jnp.einsum('kij,kic->kjc', res.astype(jnp.float32), basis_tiles[rows].astype(jnp.float32))
            return (total.at[cols].add(contrib), None)
        start = jnp.zeros((ITEMS // TILE, TILE, VECS), jnp.float32)
        total, _ = lax.scan(step, start, jnp.arange(N_ROW * N_COL, dtype=jnp.int32))
        return total.reshape(ITEMS, VECS)
    basis_items = start_vectors
    for step_index in range(2):
        users_q = orthonormal(forward(basis_items))
        user_basis = users_q.astype(jnp.bfloat16)
        items_p = orthonormal(backward(user_basis))
        basis_items = items_p.astype(jnp.bfloat16)
    return (users_q * jnp.sqrt(jnp.float32(USERS)), items_p * jnp.sqrt(jnp.float32(ITEMS)))
```

```python
import jax
import jax.numpy as jnp
from jax import lax
from jax.experimental import pallas as pl
from jax.experimental.pallas import tpu as pltpu
from jax.sharding import Mesh, PartitionSpec as P

F32 = jnp.float32
BF16 = jnp.bfloat16
TILE = 128
GROUP = 4
SIZES = {"y": 4, "core": 2, "z": 8, "x": 4}
VMEM = pl.BlockSpec(memory_space=pltpu.VMEM)
SMEM = pl.BlockSpec(memory_space=pltpu.SMEM)


def hop(value, axis, distance):
    size = SIZES[axis]
    return lax.ppermute(value, axis, [(i, (i + distance) % size) for i in range(size)])


def gather_axis(value, axis):
    return jnp.stack([value] + [hop(value, axis, d) for d in range(1, SIZES[axis])])


def sum_axis(value, axis):
    total = value
    for part in [hop(value, axis, d) for d in range(1, SIZES[axis])]:
        total = total + part
    return total


def scatter_axis(value, axis):
    parts = [hop(value[d], axis, d) for d in range(1, SIZES[axis])]
    total = value[0]
    for part in parts:
        total = total + part
    return total


def sum_everywhere(gram):
    half = gram.shape[0] // 2
    core = lax.axis_index("core")
    mine = lax.dynamic_slice_in_dim(gram, core * half, half, 0)
    other = lax.dynamic_slice_in_dim(gram, (1 - core) * half, half, 0)
    part = mine + hop(other, "core", 1)
    for axis in ("y", "x", "z"):
        part = sum_axis(part, axis)
    back = hop(part, "core", 1)
    first = jnp.where(core == 0, part, back)
    second = jnp.where(core == 0, back, part)
    return jnp.concatenate([first, second], axis=0)


def gather_z(value):
    wide = jnp.broadcast_to(value[None], (SIZES["z"],) + value.shape)
    return lax.all_to_all(wide, "z", 0, 0, tiled=True)


def scatter_z(value):
    return lax.all_to_all(value, "z", 0, 0, tiled=True).sum(axis=0)


def residual_kernel(count, left_at, right_at, left, right, ratings, out):
    groups = (count[0] + GROUP - 1) // GROUP

    @pl.loop(0, groups)
    def _(g):
        for u in range(GROUP):
            k = g * GROUP + u
            product = lax.dot_general(
                left[left_at[k]],
                right[right_at[k]],
                (((0,), (0,)), ((), ())),
                preferred_element_type=F32,
            )
            value = product - ratings[k].astype(F32)
            out[k] = jnp.where(k < count[0], value, 0.0).astype(BF16)


def forward_kernel(count, from_at, to_at, residual, basis, out):
    out[...] = jnp.zeros_like(out)
    groups = (count[0] + GROUP - 1) // GROUP

    @pl.loop(0, groups)
    def _(g):
        slots = [g * GROUP + u for u in range(GROUP)]
        parts = [
            jnp.dot(residual[k], basis[from_at[k]], preferred_element_type=F32) for k in slots
        ]
        for k, part in zip(slots, parts):
            out[to_at[k]] += part


def backward_kernel(count, from_at, to_at, residual, basis, out):
    out[...] = jnp.zeros_like(out)
    groups = (count[0] + GROUP - 1) // GROUP

    @pl.loop(0, groups)
    def _(g):
        slots = [g * GROUP + u for u in range(GROUP)]
        parts = [
            lax.dot_general(
                residual[k],
                basis[from_at[k]],
                (((0,), (0,)), ((), ())),
                preferred_element_type=F32,
            )
            for k in slots
        ]
        for k, part in zip(slots, parts):
            out[to_at[k]] += part


def inverse_factor_kernel(gram, out):
    size = gram.shape[0]
    panels = size // 8
    sub = lax.broadcasted_iota(jnp.int32, (8, size), 0)
    lane = lax.broadcasted_iota(jnp.int32, (8, size), 1)
    left = [gram[8 * k : 8 * k + 8, :] for k in range(panels)]
    right = [jnp.where(lane == sub + 8 * k, 1.0, 0.0).astype(F32) for k in range(panels)]
    for j in range(size):
        k, i = divmod(j, 8)
        row_left = left[k][i : i + 1, :]
        row_right = right[k][i : i + 1, :]
        scale = 1.0 / row_left[:, j : j + 1]
        row_left = row_left * scale
        row_right = row_right * scale
        for m in range(k, panels):
            factor = left[m][:, j : j + 1]
            if m == k:
                if i == 7:
                    continue
                factor = jnp.where(sub[:, :1] > i, factor, 0.0)
            left[m] = left[m] - factor * row_left
            right[m] = right[m] - factor * row_right
    for k in range(panels):
        pivot = jnp.sum(jnp.where(lane == sub + 8 * k, left[k], 0.0), axis=1, keepdims=True)
        out[8 * k : 8 * k + 8, :] = right[k] * (1.0 / jnp.sqrt(pivot))


def split(value):
    high = value.astype(BF16)
    return high, (value - high.astype(F32)).astype(BF16)


def apply_kernel(value, inverse, out):
    inverse_high, inverse_low = split(inverse[...])
    dims = (((1,), (1,)), ((), ()))

    @pl.loop(0, value.shape[0])
    def _(t):
        high, low = split(value[t])
        dot = lambda a, b: lax.dot_general(a, b, dims, preferred_element_type=F32)
        out[t] = (
            dot(high, inverse_high) + (dot(high, inverse_low) + dot(low, inverse_high))
        ).astype(BF16)


def call(kernel, shape, dtype, name, flops, scalars, arrays):
    return pl.pallas_call(
        kernel,
        out_shape=jax.ShapeDtypeStruct(shape, dtype),
        in_specs=[SMEM] * len(scalars) + [VMEM] * len(arrays),
        out_specs=VMEM,
        name=name,
        cost_estimate=pl.CostEstimate(
            flops=flops, bytes_accessed=sum(a.size * a.dtype.itemsize for a in arrays),
            transcendentals=0,
        ),
        compiler_params=pltpu.CompilerParams(vmem_limit_bytes=40 * 1024 * 1024),
    )(*scalars, *arrays)


def gram_of(block):
    return jnp.dot(
        block.T, block, precision=lax.Precision.HIGHEST, preferred_element_type=jnp.float32
    )


def times_inverse(block, inverse):
    return jnp.dot(
        block, inverse.T, precision=lax.Precision.HIGHEST, preferred_element_type=jnp.float32
    )


def shards(user_factors, item_factors, start_vectors, ratings, tile_rows, tile_cols, tile_count):
    slots = ratings.shape[2]
    rank = user_factors.shape[1]
    y, core = lax.axis_index("y"), lax.axis_index("core")
    z, x = lax.axis_index("z"), lax.axis_index("x")
    rows, cols = tile_rows[0, 0], tile_cols[0, 0]
    count = tile_count[0]
    tiles = slots * TILE * TILE
    row_z, row_x = rows // 4, rows % 4
    col_y, col_core, col_i = cols // 4, (cols // 2) % 2, cols % 2
    rows_in = ((x - row_x) % 4) * 8 + row_z
    rows_out = ((row_x - x) % 4) * 8 + row_z
    cols_in = ((core - col_core) % 2) * 8 + ((y - col_y) % 4) * 2 + col_i
    cols_out = ((col_core - core) % 2) * 8 + ((col_y - y) % 4) * 2 + col_i

    def gather_items(share):
        share = share.reshape((2, -1) + share.shape[1:]) if share.shape[0] != 2 else share
        block = gather_axis(gather_axis(share, "y"), "core")
        return block.reshape((16,) + share.shape[1:])

    def gather_users(share):
        block = gather_axis(gather_z(share), "x")
        return block.reshape((32,) + share.shape)

    users = gather_users(user_factors.T)
    items = gather_items(jnp.transpose(item_factors.reshape(2, TILE, rank), (0, 2, 1)))
    basis = gather_items(start_vectors)
    residual = call(
        residual_kernel, (slots, TILE, TILE), BF16, "residual", 2 * tiles * rank,
        (count, rows_in, cols_in), (users, items, ratings[0, 0]),
    )
    users_total = user_factors.shape[0] * 256
    items_total = item_factors.shape[0] * 256
    for step in range(2):
        partial = call(
            forward_kernel, (32, TILE, TILE), F32, "forward", 2 * tiles * TILE,
            (count, cols_in, rows_out), (residual, basis),
        )
        share = scatter_z(scatter_axis(partial.reshape(4, 8, TILE, TILE), "x"))
        gram = sum_everywhere(gram_of(share))
        block = gather_users(share)
        inverse = call(inverse_factor_kernel, (TILE, TILE), F32, "factor", TILE**3, (), (gram,))
        basis = call(
            apply_kernel, (32, TILE, TILE), BF16, "apply_users", 32 * 6 * TILE**3, (),
            (block, inverse),
        )
        if step == 1:
            user_out = times_inverse(share, inverse) * jnp.sqrt(F32(users_total))
        partial = call(
            backward_kernel, (16, TILE, TILE), F32, "backward", 2 * tiles * TILE,
            (count, rows_in, cols_out), (residual, basis),
        )
        partial = partial.reshape(2, 4, 2, TILE, TILE)
        share = scatter_axis(scatter_axis(partial, "core"), "y")
        gram = sum_everywhere(gram_of(share.reshape(2 * TILE, TILE)))
        if step == 0:
            block = gather_items(share)
        inverse = call(inverse_factor_kernel, (TILE, TILE), F32, "factor", TILE**3, (), (gram,))
        if step == 0:
            basis = call(
                apply_kernel, (16, TILE, TILE), BF16, "apply_items", 16 * 6 * TILE**3, (),
                (block, inverse),
            )
        else:
            item_out = times_inverse(share.reshape(2 * TILE, TILE), inverse) * jnp.sqrt(
                F32(items_total)
            )
    return user_out, item_out


def solution(mesh):
    fine = Mesh(mesh.devices.reshape(4, 2, 8, 4), ("y", "core", "z", "x"))
    row, col = ("y", "core"), ("z", "x")
    in_specs = (
        P(row + col, None),
        P(col + row, None),
        P(col + row, None),
        P(row, col, None, None, None),
        P(row, col, None),
        P(row, col, None),
        P(row, col),
    )
    out_specs = (P(row + col, None), P(col + row, None))
    return jax.shard_map(shards, mesh=fine, in_specs=in_specs, out_specs=out_specs, check_vma=False)
```

```python
import jax
import jax.numpy as jnp
from jax import lax
from jax.experimental import pallas as pl
from jax.experimental.pallas import tpu as pltpu
from jax.sharding import Mesh, PartitionSpec as P

F32 = jnp.float32
BF16 = jnp.bfloat16
TILE = 128
GROUP = 8
Z_TYPE = BF16
FIRST_LIMIT = 60
SIZES = {"y": 4, "core": 2, "z": 8, "x": 4}
VMEM = pl.BlockSpec(memory_space=pltpu.VMEM)
SMEM = pl.BlockSpec(memory_space=pltpu.SMEM)
HBM = pl.BlockSpec(memory_space=pltpu.HBM)


def hop(value, axis, distance):
    size = SIZES[axis]
    return lax.ppermute(value, axis, [(i, (i + distance) % size) for i in range(size)])


def gather_axis(value, axis):
    return [value] + [hop(value, axis, d) for d in range(1, SIZES[axis])]


def sum_axis(value, axis):
    total = value
    for part in [hop(value, axis, d) for d in range(1, SIZES[axis])]:
        total = total + part
    return total


def scatter_axis(value, axis):
    parts = [hop(value[d], axis, d) for d in range(1, SIZES[axis])]
    total = value[0]
    for part in parts:
        total = total + part
    return total


def gather_z(value):
    wide = jnp.broadcast_to(value[None], (SIZES["z"],) + value.shape)
    return lax.all_to_all(wide, "z", 0, 0, tiled=True)


CHUNKS = 4
COUNT_CORE, ROWS_IN, COLS_IN, ROWS_OUT, COLS_OUT = range(5)


def slot_groups(first, last, body):
    @pl.loop(first, last)
    def _(g):
        body([g * GROUP + u for u in range(GROUP)])


def run_all(copies):
    for copy in copies:
        copy.start()
    for copy in copies:
        copy.wait()


def first_kernel(
    places, u0, u1, u2, u3, item0, item1, ratings,
    residual, o0, o1, o2, o3, users, items, rated, total, cut, sems,
):
    count = places[COUNT_CORE, 0]
    chunk = rated.shape[0] // CHUNKS
    copies = [
        pltpu.make_async_copy(ref, users.at[pl.ds(8 * d, 8)], sems.at[d])
        for d, ref in enumerate((u0, u1, u2, u3))
    ]
    copies += [
        pltpu.make_async_copy(ref, items.at[pl.ds(8 * d, 8)], sems.at[4 + d])
        for d, ref in enumerate((item0, item1))
    ]
    chunks = [
        pltpu.make_async_copy(
            ratings.at[pl.ds(c * chunk, chunk)], rated.at[pl.ds(c * chunk, chunk)], sems.at[6 + c]
        )
        for c in range(CHUNKS)
    ]
    for copy in copies + chunks:
        copy.start()
    total[...] = jnp.zeros_like(total)
    for copy in copies:
        copy.wait()
    rank = users.shape[1]

    def body(slots):
        tiles = []
        for k in slots:
            product = lax.dot_general(
                users[places[ROWS_IN, k]],
                items[places[COLS_IN, k], :rank],
                (((0,), (0,)), ((), ())),
                preferred_element_type=F32,
            )
            value = jnp.where(k < count, product - rated[k].astype(F32), 0.0)
            tiles.append(value.astype(BF16))
        for k, tile in zip(slots, tiles):
            residual[k] = tile
        parts = [
            jnp.dot(tile, items[places[COLS_IN, k], rank:], preferred_element_type=F32)
            for k, tile in zip(slots, tiles)
        ]
        for k, part in zip(slots, parts):
            total[places[ROWS_OUT, k]] += part

    groups = (count + GROUP - 1) // GROUP
    per = chunk // GROUP
    for c in range(CHUNKS):
        chunks[c].wait()
        slot_groups(jnp.minimum(c * per, groups), jnp.minimum((c + 1) * per, groups), body)
    copies = [pltpu.make_async_copy(total.at[pl.ds(0, 8)], o0, sems.at[0])]
    copies[0].start()
    cut[...] = total[8:].astype(BF16)
    for d, ref in enumerate((o1, o2, o3)):
        copies.append(pltpu.make_async_copy(cut.at[pl.ds(8 * d, 8)], ref, sems.at[1 + d]))
        copies[-1].start()
    for copy in copies:
        copy.wait()


def split_into(pair, refs):
    depth = refs[0].shape[0]
    for d, ref in enumerate(refs):
        for i in range(depth):
            value = ref[i]
            high = value.astype(BF16)
            pair[d * depth + i, :TILE] = high
            pair[d * depth + i, TILE:] = (value - high.astype(F32)).astype(BF16)


def gram_from(pair):
    def step(t, total):
        both = pair[t]
        turned = jnp.concatenate([both[TILE:], both[:TILE]], axis=0)
        return total + lax.dot_general(
            both,
            jnp.concatenate([both, turned], axis=1),
            (((0,), (0,)), ((), ())),
            preferred_element_type=F32,
        )

    tiles = pair.shape[0]
    total = lax.fori_loop(0, tiles, step, jnp.zeros((TILE, 2 * TILE), F32), unroll=4)
    return total[:, :TILE] + total[:, TILE:]


def gram_of_blocks(blocks):
    total = jnp.zeros((TILE, TILE), F32)
    for block in blocks:

        def step(t, total):
            tiles = block[pl.ds(2 * t, 2)].reshape(2 * TILE, TILE)
            return total + lax.dot_general(
                tiles, tiles, (((0,), (0,)), ((), ())), preferred_element_type=F32
            )

        total = lax.fori_loop(0, block.shape[0] // 2, step, total, unroll=True)
    return total


def add_products(axis, places, from_row, to_row, residual, basis, total):
    repeat = basis.shape[1] // TILE
    total[...] = jnp.zeros_like(total)

    def body(slots):
        parts = []
        for k in slots:
            tile = residual[k]
            tile = tile if repeat == 1 else jnp.concatenate([tile, tile], axis=axis)
            parts.append(
                lax.dot_general(
                    tile, basis[places[from_row, k]], (((axis,), (0,)), ((), ())),
                    preferred_element_type=F32,
                )
            )
        for k, part in zip(slots, parts):
            total[places[to_row, k]] += part

    slot_groups(0, (places[COUNT_CORE, 0] + GROUP - 1) // GROUP, body)


def backward_kernel(places, residual, b0, b1, b2, b3, mine, other, basis, total, gram, sems):
    blocks = (b0, b1, b2, b3)
    for d, ref in enumerate(blocks):
        basis[8 * d : 8 * d + 8] = ref[...]
    add_products(0, places, ROWS_IN, COLS_OUT, residual, basis, total)
    gram[...] = gram_of_blocks(blocks)
    core = places[COUNT_CORE, 1]
    half = TILE // 2
    copies = []
    for d, (ref, who) in enumerate(((mine, core), (other, 1 - core))):
        for t in range(8):
            copies.append(
                pltpu.make_async_copy(
                    total.at[8 * d + t], ref.at[pl.ds(TILE * t, TILE)], sems.at[9 * d + t]
                )
            )
        copies.append(
            pltpu.make_async_copy(
                gram.at[pl.ds(pl.multiple_of(who * half, half), half)],
                ref.at[pl.ds(8 * TILE, half)],
                sems.at[9 * d + 8],
            )
        )
    run_all(copies)


def forward_kernel(
    places, residual, b0, b1, b2, b3, b4, b5, b6, b7,
    own_gram, o0, o1, o2, o3, pair, total, gram, cut, sems,
):
    split_into(pair, (b0, b1, b2, b3, b4, b5, b6, b7))
    add_products(1, places, COLS_IN, ROWS_OUT, residual, pair, total)
    copies = [pltpu.make_async_copy(total.at[pl.ds(0, 8)], o0, sems.at[0])]
    copies[0].start()
    gram[...] = gram_from(pair)
    half = TILE // 2
    mine = gram[pl.ds(pl.multiple_of(places[COUNT_CORE, 1] * half, half), half)]
    own_gram[...] = mine
    high = mine.astype(BF16)
    low = (mine - high.astype(F32)).astype(BF16)
    for d, ref in enumerate((o1, o2, o3)):
        for t in range(8):
            cut[d, TILE * t : TILE * (t + 1)] = total[8 + 8 * d + t].astype(BF16)
        cut[d, 8 * TILE : 8 * TILE + half] = high
        cut[d, 8 * TILE + half :] = low
        copies.append(pltpu.make_async_copy(cut.at[d], ref, sems.at[1 + d]))
        copies[-1].start()
    for copy in copies:
        copy.wait()


def inverse_factor_kernel(gram, out):
    size = gram.shape[0]
    panels = size // 8
    wide = (8, size)
    sub = lax.broadcasted_iota(jnp.int32, wide, 0)
    lane = lax.broadcasted_iota(jnp.int32, wide, 1)
    left = [gram[8 * k : 8 * k + 8, :] for k in range(panels)]
    on_diagonal = [lane == sub + 8 * k for k in range(panels)]
    diagonal = sum(jnp.where(on_diagonal[k], left[k], 0.0) for k in range(panels))
    column_scale = 1.0 / jnp.sqrt(jnp.sum(diagonal, axis=0, keepdims=True))
    for k in range(panels):
        row_scale = jnp.sum(jnp.where(on_diagonal[k], column_scale, 0.0), axis=1, keepdims=True)
        left[k] = left[k] * row_scale * column_scale
    right = [jnp.where(on_diagonal[k], 1.0, 0.0).astype(F32) for k in range(panels)]
    for k in range(panels):
        columns = {
            m: [jnp.broadcast_to(left[m][:, 8 * k + j : 8 * k + j + 1], wide) for j in range(8)]
            for m in range(k, panels)
        }
        for i in (0, 2, 4, 6):
            top = columns[k][i][i : i + 1]
            side = columns[k][i + 1][i : i + 1]
            low = columns[k][i + 1][i + 1 : i + 2]
            scale = 1.0 / (top * low - side * side)

            def solve(panel):
                first, second = panel[i : i + 1], panel[i + 1 : i + 2]
                return (low * first - side * second) * scale, (top * second - side * first) * scale

            left_rows, right_rows = solve(left[k]), solve(right[k])
            column_rows = {j: solve(columns[k][j]) for j in range(i + 2, 8)}
            for m in range(k, panels):
                if m == k and i == 6:
                    continue
                c0, c1 = columns[m][i], columns[m][i + 1]
                if m == k:
                    c0, c1 = jnp.where(sub > i + 1, c0, 0.0), jnp.where(sub > i + 1, c1, 0.0)
                left[m] = left[m] - (c0 * left_rows[0] + c1 * left_rows[1])
                right[m] = right[m] - (c0 * right_rows[0] + c1 * right_rows[1])
                for j in range(i + 2, 8):
                    rows = column_rows[j]
                    columns[m][j] = columns[m][j] - (c0 * rows[0] + c1 * rows[1])
    odd = sub % 2 == 1
    for k in range(panels):
        pivot = jnp.sum(jnp.where(on_diagonal[k], left[k], 0.0), axis=1, keepdims=True)
        beside = jnp.where(odd & (lane == sub + 8 * k - 1), left[k], 0.0)
        pivot = jnp.broadcast_to(pivot, wide)
        beside = jnp.broadcast_to(jnp.sum(beside, axis=1, keepdims=True), wide)
        factor = jnp.where(odd, beside / pltpu.roll(pivot, 1, 0), 0.0)
        rows = right[k] - factor * pltpu.roll(right[k], 1, 0)
        out[8 * k : 8 * k + 8, :] = rows * (1.0 / jnp.sqrt(pivot - factor * beside)) * column_scale


def call(kernel, outs, name, flops, ins, arrays, scratch, limit=40):
    return pl.pallas_call(
        kernel,
        out_shape=[jax.ShapeDtypeStruct(shape, dtype) for shape, dtype, _ in outs],
        in_specs=ins,
        out_specs=[place for _, _, place in outs],
        scratch_shapes=scratch,
        name=name,
        cost_estimate=pl.CostEstimate(
            flops=flops,
            bytes_accessed=sum(a.size * a.dtype.itemsize for a in arrays),
            transcendentals=0,
        ),
        compiler_params=pltpu.CompilerParams(vmem_limit_bytes=limit * 1024 * 1024),
    )(*arrays)


def gram_of(block):
    return jnp.dot(
        block.T, block, precision=lax.Precision.HIGHEST, preferred_element_type=jnp.float32
    )


def times_inverse(block, inverse):
    return jnp.dot(
        block, inverse.T, precision=lax.Precision.HIGHEST, preferred_element_type=jnp.float32
    )


def split(value):
    high = value.astype(BF16)
    return high, (value - high.astype(F32)).astype(BF16)


def inverse_factor(gram):
    return call(
        inverse_factor_kernel, [((TILE, TILE), F32, VMEM)], "factor", 4 * TILE**3, [VMEM], (gram,), []
    )[0]


def both_halves(half):
    core = lax.axis_index("core")
    back = hop(half, "core", 1)
    return jnp.concatenate([jnp.where(core == 0, half, back), jnp.where(core == 0, back, half)])


def own_half(gram, core):
    half = gram.shape[0] // 2
    return lax.dynamic_slice_in_dim(gram, core * half, half, 0)


def shards(user_factors, item_factors, start_vectors, ratings, tile_rows, tile_cols, tile_count):
    slots = ratings.shape[2]
    rank = user_factors.shape[1]
    y, core = lax.axis_index("y"), lax.axis_index("core")
    x = lax.axis_index("x")
    rows, cols = tile_rows[0, 0], tile_cols[0, 0]
    work = slots * TILE * TILE
    row_z, row_x = rows // 4, rows % 4
    col_y, col_core, col_i = cols // 4, (cols // 2) % 2, cols % 2
    col_turn = ((core - col_core) % 2) * 8 + col_i
    slot = jnp.arange(slots, dtype=jnp.int32)
    places = jnp.stack(
        [
            jnp.where(slot == 0, tile_count[0, 0], core),
            ((x - row_x) % 4) * 8 + row_z,
            col_turn + ((y - col_y) % 4) * 2,
            ((row_x - x) % 4) * 8 + row_z,
            col_turn + ((col_y - y) % 4) * 2,
        ]
    )

    factors = jnp.transpose(item_factors.reshape(2, TILE, rank), (0, 2, 1))
    item_share = jnp.concatenate([factors, start_vectors.reshape(2, TILE, TILE)], axis=1)
    items = jnp.stack(gather_axis(item_share, "y")).reshape(8, rank + TILE, TILE)
    items = gather_axis(items, "core")
    users = gather_axis(gather_z(user_factors.T), "x")
    own_sums = ((8, TILE, TILE), F32, HBM)
    item_sums = [((8 * TILE + TILE // 2, TILE), F32, HBM)] * 2
    residual, *partial = call(
        first_kernel, [((slots, TILE, TILE), BF16, VMEM), own_sums] + [((8, TILE, TILE), BF16, HBM)] * 3, "first",
        2 * work * (rank + TILE), [SMEM] + [HBM] * 7, (places, *users, *items, ratings[0, 0]),
        [
            pltpu.VMEM((32, rank, TILE), BF16),
            pltpu.VMEM((16, rank + TILE, TILE), BF16),
            pltpu.VMEM((slots, TILE, TILE), BF16),
            pltpu.VMEM((32, TILE, TILE), F32),
            pltpu.VMEM((24, TILE, TILE), BF16),
            pltpu.SemaphoreType.DMA((6 + CHUNKS,)),
        ],
        FIRST_LIMIT,
    )
    for step in range(2):
        parts = [hop(partial[d], "x", d) for d in range(1, 4)]
        message = partial[0]
        for part in parts:
            tiles = part.reshape(-1, TILE)[: 8 * TILE].reshape(8, TILE, TILE)
            message = message + tiles.astype(F32)
        message = message.astype(Z_TYPE)
        if step == 1:
            half = own_gram
            for part in parts:
                half = half + part[8 * TILE : -(TILE // 2)].astype(F32)
                half = half + part[-(TILE // 2) :].astype(F32)
            high, low = split(half)
            below = jnp.concatenate([high, low]) if Z_TYPE == BF16 else half
            below = jnp.broadcast_to(below[None], (8,) + below.shape)
            message = jnp.concatenate([message, below], axis=1)
        summed = lax.all_to_all(message, "z", 0, 0, tiled=True).astype(F32).sum(axis=0)
        user_share = summed[:TILE]
        if step == 1:
            half = summed[TILE : TILE + TILE // 2]
            if Z_TYPE == BF16:
                half = half + summed[-(TILE // 2) :]
            user_share = times_inverse(user_share, inverse_factor(both_halves(half)))
        user_blocks = gather_axis(gather_z(user_share.astype(BF16)), "x")
        mine, other = call(
            backward_kernel, item_sums, "backward", 4 * work * TILE,
            [SMEM] + [VMEM] * 5, (places, residual, *user_blocks),
            [
                pltpu.VMEM((32, TILE, TILE), BF16),
                pltpu.VMEM((16, TILE, TILE), F32),
                pltpu.VMEM((TILE, TILE), F32),
                pltpu.SemaphoreType.DMA((18,)),
            ],
        )
        mine = mine + hop(other, "core", 1)
        rows_of = 2 * TILE
        messages = [
            jnp.concatenate([mine[rows_of * d : rows_of * (d + 1)], mine[4 * rows_of :]])
            for d in range(4)
        ]
        summed = scatter_axis(messages, "y")
        inverse = inverse_factor(both_halves(summed[rows_of:]))
        item_share = times_inverse(summed[:rows_of], inverse)
        if step == 0:
            blocks = gather_axis(item_share.reshape(2, TILE, TILE), "y")
            blocks = blocks + [hop(block, "core", 1) for block in blocks]
            own_gram, *partial = call(
                forward_kernel,
                [((TILE // 2, TILE), F32, VMEM), own_sums] + [((9 * TILE, TILE), BF16, HBM)] * 3,
                "forward", 4 * work * TILE, [SMEM] + [VMEM] * 9, (places, residual, *blocks),
                [
                    pltpu.VMEM((16, 2 * TILE, TILE), BF16),
                    pltpu.VMEM((32, TILE, TILE), F32),
                    pltpu.VMEM((TILE, TILE), F32),
                    pltpu.VMEM((3, 9 * TILE, TILE), BF16),
                    pltpu.SemaphoreType.DMA((4,)),
                ],
            )
    gram = gram_of(item_share)
    half = own_half(gram, core) + hop(own_half(gram, 1 - core), "core", 1)
    half = gather_z(sum_axis(sum_axis(half, "y"), "x")).sum(axis=0)
    item_inverse = inverse_factor(both_halves(half))
    users_total = user_factors.shape[0] * 256
    items_total = item_factors.shape[0] * 256
    user_out = times_inverse(user_share, inverse) * jnp.sqrt(F32(users_total))
    item_out = times_inverse(item_share, item_inverse) * jnp.sqrt(F32(items_total))
    return user_out, item_out


def solution(mesh):
    fine = Mesh(mesh.devices.reshape(4, 2, 8, 4), ("y", "core", "z", "x"))
    row, col = ("y", "core"), ("z", "x")
    in_specs = (
        P(row + col, None),
        P(col + row, None),
        P(col + row, None),
        P(row, col, None, None, None),
        P(row, col, None),
        P(row, col, None),
        P(row, col),
    )
    out_specs = (P(row + col, None), P(col + row, None))
    return jax.shard_map(shards, mesh=fine, in_specs=in_specs, out_specs=out_specs, check_vma=False)
```

```python
import jax
import jax.numpy as jnp
from jax import lax
from jax.experimental import pallas as pl
from jax.experimental.pallas import tpu as pltpu
from jax.sharding import Mesh, PartitionSpec as P

F32 = jnp.float32
BF16 = jnp.bfloat16
TILE = 128
GROUP = 24
Z_TYPE = BF16
FIRST_LIMIT = 60
SIZES = {"y": 4, "core": 2, "z": 8, "x": 4}
VMEM = pl.BlockSpec(memory_space=pltpu.VMEM)
SMEM = pl.BlockSpec(memory_space=pltpu.SMEM)
HBM = pl.BlockSpec(memory_space=pltpu.HBM)


def hop(value, axis, distance):
    size = SIZES[axis]
    return lax.ppermute(value, axis, [(i, (i + distance) % size) for i in range(size)])


def gather_axis(value, axis):
    return [value] + [hop(value, axis, d) for d in range(1, SIZES[axis])]


def sum_axis(value, axis):
    total = value
    for part in [hop(value, axis, d) for d in range(1, SIZES[axis])]:
        total = total + part
    return total


def gather_z(value):
    wide = jnp.broadcast_to(value[None], (SIZES["z"],) + value.shape)
    return lax.all_to_all(wide, "z", 0, 0, tiled=True)


CHUNKS = 4
COUNT_CORE, ROWS_IN, COLS_IN, ROWS_OUT, COLS_OUT, START_IN = range(6)


def slot_groups(first, last, body):
    @pl.loop(first, last)
    def _(g):
        body([g * GROUP + u for u in range(GROUP)])


def run_all(copies):
    for copy in copies:
        copy.start()
    for copy in copies:
        copy.wait()


def first_kernel(
    places, u0, u1, u2, u3, s0, s1, s2, s3, ratings,
    residual, o0, o1, o2, o3, users, items, rated, total, cut, sems,
):
    count = places[COUNT_CORE, 0]
    chunk = rated.shape[0] // CHUNKS
    copies = [
        pltpu.make_async_copy(ref, users.at[pl.ds(8 * d, 8)], sems.at[d])
        for d, ref in enumerate((u0, u1, u2, u3))
    ]
    copies += [
        pltpu.make_async_copy(ref, items.at[pl.ds(4 * d, 4)], sems.at[4 + d])
        for d, ref in enumerate((s0, s1, s2, s3))
    ]
    chunks = [
        pltpu.make_async_copy(
            ratings.at[pl.ds(c * chunk, chunk)], rated.at[pl.ds(c * chunk, chunk)], sems.at[8 + c]
        )
        for c in range(CHUNKS)
    ]
    for copy in copies + chunks:
        copy.start()
    total[...] = jnp.zeros_like(total)
    for copy in copies:
        copy.wait()
    rank = users.shape[1]

    def body(slots):
        tiles = []
        for k in slots:
            product = lax.dot_general(
                users[places[ROWS_IN, k]],
                items[places[START_IN, k], :rank],
                (((0,), (0,)), ((), ())),
                preferred_element_type=F32,
            )
            value = jnp.where(k < count, product - rated[k].astype(F32), 0.0)
            tiles.append(value.astype(BF16))
        for k, tile in zip(slots, tiles):
            residual[k] = tile
        parts = [
            jnp.dot(tile, items[places[START_IN, k], rank:], preferred_element_type=F32)
            for k, tile in zip(slots, tiles)
        ]
        for k, part in zip(slots, parts):
            total[places[ROWS_OUT, k]] += part

    groups = (count + GROUP - 1) // GROUP
    per = chunk // GROUP
    for c in range(CHUNKS):
        chunks[c].wait()
        slot_groups(jnp.minimum(c * per, groups), jnp.minimum((c + 1) * per, groups), body)
    copies = [pltpu.make_async_copy(total.at[pl.ds(0, 8)], o0, sems.at[0])]
    copies[0].start()
    cut[...] = total[8:].astype(BF16)
    for d, ref in enumerate((o1, o2, o3)):
        copies.append(pltpu.make_async_copy(cut.at[pl.ds(8 * d, 8)], ref, sems.at[1 + d]))
        copies[-1].start()
    for copy in copies:
        copy.wait()


def gram_of_blocks(blocks):
    total = jnp.zeros((TILE, TILE), F32)
    for block in blocks:

        def step(t, total):
            tiles = block[pl.ds(2 * t, 2)].reshape(2 * TILE, TILE)
            return total + lax.dot_general(
                tiles, tiles, (((0,), (0,)), ((), ())), preferred_element_type=F32
            )

        total = lax.fori_loop(0, block.shape[0] // 2, step, total, unroll=True)
    return total


def add_products(axis, places, from_row, to_row, residual, basis, total):
    total[...] = jnp.zeros_like(total)

    def body(slots):
        parts = []
        for k in slots:
            parts.append(
                lax.dot_general(
                    residual[k], basis[places[from_row, k]], (((axis,), (0,)), ((), ())),
                    preferred_element_type=F32,
                )
            )
        for k, part in zip(slots, parts):
            total[places[to_row, k]] += part

    slot_groups(0, (places[COUNT_CORE, 0] + GROUP - 1) // GROUP, body)


def backward_kernel(places, residual, b0, b1, b2, b3, mine, other, basis, total, gram, sems):
    blocks = (b0, b1, b2, b3)
    for d, ref in enumerate(blocks):
        basis[8 * d : 8 * d + 8] = ref[...]
    add_products(0, places, ROWS_IN, COLS_OUT, residual, basis, total)
    gram[...] = gram_of_blocks(blocks)
    core = places[COUNT_CORE, 1]
    half = TILE // 2
    copies = []
    for d, (ref, who) in enumerate(((mine, core), (other, 1 - core))):
        for t in range(8):
            copies.append(
                pltpu.make_async_copy(
                    total.at[8 * d + t], ref.at[pl.ds(TILE * t, TILE)], sems.at[9 * d + t]
                )
            )
        copies.append(
            pltpu.make_async_copy(
                gram.at[pl.ds(pl.multiple_of(who * half, half), half)],
                ref.at[pl.ds(8 * TILE, half)],
                sems.at[9 * d + 8],
            )
        )
    run_all(copies)


def forward_kernel(
    places, residual, b0, b1, b2, b3, b4, b5, b6, b7,
    own_gram, o0, o1, o2, o3, basis, total, gram, cut, sems,
):
    blocks = (b0, b1, b2, b3, b4, b5, b6, b7)
    for d, ref in enumerate(blocks):
        basis[2 * d : 2 * d + 2] = ref[...]
    add_products(1, places, COLS_IN, ROWS_OUT, residual, basis, total)
    copies = [pltpu.make_async_copy(total.at[pl.ds(0, 8)], o0, sems.at[0])]
    copies[0].start()
    gram[...] = gram_of_blocks(blocks)
    half = TILE // 2
    mine = gram[pl.ds(pl.multiple_of(places[COUNT_CORE, 1] * half, half), half)]
    own_gram[...] = mine
    high = mine.astype(BF16)
    low = (mine - high.astype(F32)).astype(BF16)
    for d, ref in enumerate((o1, o2, o3)):
        for t in range(8):
            cut[d, TILE * t : TILE * (t + 1)] = total[8 + 8 * d + t].astype(BF16)
        cut[d, 8 * TILE : 8 * TILE + half] = high
        cut[d, 8 * TILE + half :] = low
        copies.append(pltpu.make_async_copy(cut.at[d], ref, sems.at[1 + d]))
        copies[-1].start()
    for copy in copies:
        copy.wait()


def inverse_factor_kernel(gram, out):
    size = gram.shape[0]
    panels = size // 8
    wide = (8, size)
    sub = lax.broadcasted_iota(jnp.int32, wide, 0)
    lane = lax.broadcasted_iota(jnp.int32, wide, 1)
    left = [gram[8 * k : 8 * k + 8, :] for k in range(panels)]
    on_diagonal = [lane == sub + 8 * k for k in range(panels)]
    diagonal = sum(jnp.where(on_diagonal[k], left[k], 0.0) for k in range(panels))
    column_scale = 1.0 / jnp.sqrt(jnp.sum(diagonal, axis=0, keepdims=True))
    for k in range(panels):
        row_scale = jnp.sum(jnp.where(on_diagonal[k], column_scale, 0.0), axis=1, keepdims=True)
        left[k] = left[k] * row_scale * column_scale
    right = [jnp.where(on_diagonal[k], 1.0, 0.0).astype(F32) for k in range(panels)]
    for k in range(panels):
        columns = {
            m: [jnp.broadcast_to(left[m][:, 8 * k + j : 8 * k + j + 1], wide) for j in range(8)]
            for m in range(k, panels)
        }
        for i in (0, 2, 4, 6):
            top = columns[k][i][i : i + 1]
            side = columns[k][i + 1][i : i + 1]
            low = columns[k][i + 1][i + 1 : i + 2]
            scale = 1.0 / (top * low - side * side)

            def solve(panel):
                first, second = panel[i : i + 1], panel[i + 1 : i + 2]
                return (low * first - side * second) * scale, (top * second - side * first) * scale

            left_rows, right_rows = solve(left[k]), solve(right[k])
            column_rows = {j: solve(columns[k][j]) for j in range(i + 2, 8)}
            for m in range(k, panels):
                if m == k and i == 6:
                    continue
                c0, c1 = columns[m][i], columns[m][i + 1]
                if m == k:
                    c0, c1 = jnp.where(sub > i + 1, c0, 0.0), jnp.where(sub > i + 1, c1, 0.0)
                left[m] = left[m] - (c0 * left_rows[0] + c1 * left_rows[1])
                right[m] = right[m] - (c0 * right_rows[0] + c1 * right_rows[1])
                for j in range(i + 2, 8):
                    rows = column_rows[j]
                    columns[m][j] = columns[m][j] - (c0 * rows[0] + c1 * rows[1])
    odd = sub % 2 == 1
    for k in range(panels):
        pivot = jnp.sum(jnp.where(on_diagonal[k], left[k], 0.0), axis=1, keepdims=True)
        beside = jnp.where(odd & (lane == sub + 8 * k - 1), left[k], 0.0)
        pivot = jnp.broadcast_to(pivot, wide)
        beside = jnp.broadcast_to(jnp.sum(beside, axis=1, keepdims=True), wide)
        factor = jnp.where(odd, beside / pltpu.roll(pivot, 1, 0), 0.0)
        rows = right[k] - factor * pltpu.roll(right[k], 1, 0)
        out[8 * k : 8 * k + 8, :] = rows * (1.0 / jnp.sqrt(pivot - factor * beside)) * column_scale


def call(kernel, outs, name, flops, ins, arrays, scratch, limit=40):
    return pl.pallas_call(
        kernel,
        out_shape=[jax.ShapeDtypeStruct(shape, dtype) for shape, dtype, _ in outs],
        in_specs=ins,
        out_specs=[place for _, _, place in outs],
        scratch_shapes=scratch,
        name=name,
        cost_estimate=pl.CostEstimate(
            flops=flops,
            bytes_accessed=sum(a.size * a.dtype.itemsize for a in arrays),
            transcendentals=0,
        ),
        compiler_params=pltpu.CompilerParams(vmem_limit_bytes=limit * 1024 * 1024),
    )(*arrays)


def gram_of(block):
    return jnp.dot(
        block.T, block, precision=lax.Precision.HIGHEST, preferred_element_type=jnp.float32
    )


def times_inverse(block, inverse):
    return jnp.dot(
        block, inverse.T, precision=lax.Precision.HIGHEST, preferred_element_type=jnp.float32
    )


def split(value):
    high = value.astype(BF16)
    return high, (value - high.astype(F32)).astype(BF16)


def inverse_factor(gram):
    return call(
        inverse_factor_kernel, [((TILE, TILE), F32, VMEM)], "factor", 4 * TILE**3, [VMEM], (gram,), []
    )[0]


def both_halves(half):
    core = lax.axis_index("core")
    back = hop(half, "core", 1)
    return jnp.concatenate([jnp.where(core == 0, half, back), jnp.where(core == 0, back, half)])


def own_half(gram, core):
    half = gram.shape[0] // 2
    return lax.dynamic_slice_in_dim(gram, core * half, half, 0)


def shards(user_factors, item_factors, start_vectors, ratings, tile_rows, tile_cols, tile_count):
    slots = ratings.shape[2]
    rank = user_factors.shape[1]
    y, core = lax.axis_index("y"), lax.axis_index("core")
    x = lax.axis_index("x")
    rows, cols = tile_rows[0, 0], tile_cols[0, 0]
    work = slots * TILE * TILE
    row_z, row_x = rows // 4, rows % 4
    col_y, col_core, col_i = cols // 4, (cols // 2) % 2, cols % 2
    col_turn = ((core - col_core) % 2) * 8 + col_i
    slot = jnp.arange(slots, dtype=jnp.int32)
    places = jnp.stack(
        [
            jnp.where(slot == 0, tile_count[0, 0], core),
            ((x - row_x) % 4) * 8 + row_z,
            col_turn + ((y - col_y) % 4) * 2,
            ((row_x - x) % 4) * 8 + row_z,
            col_turn + ((col_y - y) % 4) * 2,
            ((y - col_y) % 4) * 4 + ((core - col_core) % 2) * 2 + col_i,
        ]
    )

    factors = jnp.transpose(item_factors.reshape(2, TILE, rank), (0, 2, 1))
    item_share = jnp.concatenate([factors, start_vectors.reshape(2, TILE, TILE)], axis=1)
    items = jnp.concatenate([item_share, hop(item_share, "core", 1)])
    items = gather_axis(items, "y")
    users = gather_axis(gather_z(user_factors.T), "x")
    own_sums = ((8, TILE, TILE), F32, HBM)
    item_sums = [((8 * TILE + TILE // 2, TILE), F32, HBM)] * 2
    residual, *partial = call(
        first_kernel, [((slots, TILE, TILE), BF16, VMEM), own_sums] + [((8, TILE, TILE), BF16, HBM)] * 3, "first",
        2 * work * (rank + TILE), [SMEM] + [HBM] * 9, (places, *users, *items, ratings[0, 0]),
        [
            pltpu.VMEM((32, rank, TILE), BF16),
            pltpu.VMEM((16, rank + TILE, TILE), BF16),
            pltpu.VMEM((slots, TILE, TILE), BF16),
            pltpu.VMEM((32, TILE, TILE), F32),
            pltpu.VMEM((24, TILE, TILE), BF16),
            pltpu.SemaphoreType.DMA((8 + CHUNKS,)),
        ],
        FIRST_LIMIT,
    )
    for step in range(2):
        parts = [hop(partial[d], "x", d) for d in range(1, 4)]
        message = partial[0]
        for part in parts:
            tiles = part.reshape(-1, TILE)[: 8 * TILE].reshape(8, TILE, TILE)
            message = message + tiles.astype(F32)
        message = message.astype(Z_TYPE)
        if step == 1:
            half = own_gram
            for part in parts:
                half = half + part[8 * TILE : -(TILE // 2)].astype(F32)
                half = half + part[-(TILE // 2) :].astype(F32)
            high, low = split(half)
            below = jnp.concatenate([high, low]) if Z_TYPE == BF16 else half
            below = jnp.broadcast_to(below[None], (8,) + below.shape)
            message = jnp.concatenate([message, below], axis=1)
        summed = lax.all_to_all(message, "z", 0, 0, tiled=True).astype(F32).sum(axis=0)
        user_share = summed[:TILE]
        if step == 1:
            half = summed[TILE : TILE + TILE // 2]
            if Z_TYPE == BF16:
                half = half + summed[-(TILE // 2) :]
            user_share = times_inverse(user_share, inverse_factor(both_halves(half)))
        user_blocks = gather_axis(gather_z(user_share.astype(BF16)), "x")
        mine, other = call(
            backward_kernel, item_sums, "backward", 4 * work * TILE,
            [SMEM] + [VMEM] * 5, (places, residual, *user_blocks),
            [
                pltpu.VMEM((32, TILE, TILE), BF16),
                pltpu.VMEM((16, TILE, TILE), F32),
                pltpu.VMEM((TILE, TILE), F32),
                pltpu.SemaphoreType.DMA((18,)),
            ],
        )
        mine = mine + hop(other, "core", 1)
        rows_of = 2 * TILE
        high, low = split(mine[4 * rows_of :])
        parts = [
            hop(
                jnp.concatenate([mine[rows_of * d : rows_of * (d + 1)].astype(BF16), high, low]),
                "y", d,
            )
            for d in range(1, 4)
        ]
        share, half = mine[:rows_of], mine[4 * rows_of :]
        for part in parts:
            share = share + part[:rows_of].astype(F32)
            half = half + (
                part[rows_of : -(TILE // 2)].astype(F32) + part[-(TILE // 2) :].astype(F32)
            )
        inverse = inverse_factor(both_halves(half))
        item_share = times_inverse(share, inverse)
        if step == 0:
            blocks = gather_axis(item_share.reshape(2, TILE, TILE).astype(BF16), "y")
            blocks = blocks + [hop(block, "core", 1) for block in blocks]
            own_gram, *partial = call(
                forward_kernel,
                [((TILE // 2, TILE), F32, VMEM), own_sums] + [((9 * TILE, TILE), BF16, HBM)] * 3,
                "forward", 4 * work * TILE, [SMEM] + [VMEM] * 9, (places, residual, *blocks),
                [
                    pltpu.VMEM((16, TILE, TILE), BF16),
                    pltpu.VMEM((32, TILE, TILE), F32),
                    pltpu.VMEM((TILE, TILE), F32),
                    pltpu.VMEM((3, 9 * TILE, TILE), BF16),
                    pltpu.SemaphoreType.DMA((4,)),
                ],
            )
    gram = gram_of(item_share)
    half = own_half(gram, core) + hop(own_half(gram, 1 - core), "core", 1)
    users_total = user_factors.shape[0] * 256
    user_out = times_inverse(user_share, inverse) * jnp.sqrt(F32(users_total))
    half, user_out = lax.optimization_barrier((sum_axis(half, "y"), user_out))
    half = gather_z(sum_axis(half, "x")).sum(axis=0)
    item_inverse = inverse_factor(both_halves(half))
    items_total = item_factors.shape[0] * 256
    item_out = times_inverse(item_share, item_inverse) * jnp.sqrt(F32(items_total))
    return user_out, item_out


def solution(mesh):
    fine = Mesh(mesh.devices.reshape(4, 2, 8, 4), ("y", "core", "z", "x"))
    row, col = ("y", "core"), ("z", "x")
    in_specs = (
        P(row + col, None),
        P(col + row, None),
        P(col + row, None),
        P(row, col, None, None, None),
        P(row, col, None),
        P(row, col, None),
        P(row, col),
    )
    out_specs = (P(row + col, None), P(col + row, None))
    return jax.shard_map(shards, mesh=fine, in_specs=in_specs, out_specs=out_specs, check_vma=False)
```

```python
import jax
import jax.numpy as jnp
from jax import lax
from jax.experimental import pallas as pl
from jax.experimental.pallas import tpu as pltpu
from jax.sharding import Mesh, PartitionSpec as P

F32 = jnp.float32
BF16 = jnp.bfloat16
TILE = 128
GROUP = 48
Z_TYPE = BF16
FIRST_LIMIT = 40
SIZES = {"y": 4, "core": 2, "z": 8, "x": 4}
VMEM = pl.BlockSpec(memory_space=pltpu.VMEM)
SMEM = pl.BlockSpec(memory_space=pltpu.SMEM)
HBM = pl.BlockSpec(memory_space=pltpu.HBM)


def hop(value, axis, distance):
    size = SIZES[axis]
    return lax.ppermute(value, axis, [(i, (i + distance) % size) for i in range(size)])


def gather_axis(value, axis):
    return [value] + [hop(value, axis, d) for d in range(1, SIZES[axis])]


def sum_axis(value, axis):
    total = value
    for part in [hop(value, axis, d) for d in range(1, SIZES[axis])]:
        total = total + part
    return total


def gather_z(value):
    wide = jnp.broadcast_to(value[None], (SIZES["z"],) + value.shape)
    return lax.all_to_all(wide, "z", 0, 0, tiled=True)


CHUNKS = 6
COUNT_CORE, ROWS_IN, COLS_IN, ROWS_OUT, COLS_OUT, START_IN = range(6)


def slot_groups(first, last, body):
    @pl.loop(first, last)
    def _(g):
        body([g * GROUP + u for u in range(GROUP)])


def run_all(copies):
    for copy in copies:
        copy.start()
    for copy in copies:
        copy.wait()


def fetch_kernel(source, out, sems):
    chunk = out.shape[0] // CHUNKS
    places = [pl.ds(c * chunk, chunk) for c in range(CHUNKS)]
    run_all(
        [
            pltpu.make_async_copy(source.at[place], out.at[place], sems.at[c])
            for c, place in enumerate(places)
        ]
    )


def first_kernel(
    places, u0, u1, u2, u3, s0, s1, s2, s3, ratings,
    residual, o0, o1, o2, o3, users, items, total, cut, sems,
):
    count = places[COUNT_CORE, 0]
    for d, ref in enumerate((u0, u1, u2, u3)):
        users[8 * d : 8 * d + 8] = ref[...]
    for d, ref in enumerate((s0, s1, s2, s3)):
        items[4 * d : 4 * d + 4] = ref[...]
    total[...] = jnp.zeros_like(total)
    rank = users.shape[1]

    def body(slots):
        tiles = []
        for k in slots:
            product = lax.dot_general(
                users[places[ROWS_IN, k]],
                items[places[START_IN, k], :rank],
                (((0,), (0,)), ((), ())),
                preferred_element_type=F32,
            )
            value = jnp.where(k < count, product - ratings[k].astype(F32), 0.0)
            tiles.append(value.astype(BF16))
        for k, tile in zip(slots, tiles):
            residual[k] = tile
        parts = [
            jnp.dot(tile, items[places[START_IN, k], rank:], preferred_element_type=F32)
            for k, tile in zip(slots, tiles)
        ]
        for k, part in zip(slots, parts):
            total[places[ROWS_OUT, k]] += part

    slot_groups(0, (count + GROUP - 1) // GROUP, body)
    copies = []
    for d, ref in enumerate((o1, o2, o3)):
        cut[8 * d : 8 * d + 8] = total[8 * d + 8 : 8 * d + 16].astype(BF16)
        copies.append(pltpu.make_async_copy(cut.at[pl.ds(8 * d, 8)], ref, sems.at[d]))
        copies[-1].start()
    o0[...] = total[:8]
    for copy in copies:
        copy.wait()


def gram_of_blocks(blocks):
    total = jnp.zeros((TILE, TILE), F32)
    for block in blocks:

        def step(t, total):
            tiles = block[pl.ds(2 * t, 2)].reshape(2 * TILE, TILE)
            return total + lax.dot_general(
                tiles, tiles, (((0,), (0,)), ((), ())), preferred_element_type=F32
            )

        total = lax.fori_loop(0, block.shape[0] // 2, step, total, unroll=True)
    return total


def add_products(axis, places, from_row, to_row, residual, basis, total):
    total[...] = jnp.zeros_like(total)

    def body(slots):
        parts = []
        for k in slots:
            parts.append(
                lax.dot_general(
                    residual[k], basis[places[from_row, k]], (((axis,), (0,)), ((), ())),
                    preferred_element_type=F32,
                )
            )
        for k, part in zip(slots, parts):
            total[places[to_row, k]] += part

    slot_groups(0, (places[COUNT_CORE, 0] + GROUP - 1) // GROUP, body)


def backward_kernel(places, residual, b0, b1, b2, b3, mine, other, basis, total, gram, sems):
    blocks = (b0, b1, b2, b3)
    for d, ref in enumerate(blocks):
        basis[8 * d : 8 * d + 8] = ref[...]
    add_products(0, places, ROWS_IN, COLS_OUT, residual, basis, total)
    gram[...] = gram_of_blocks(blocks)
    core = places[COUNT_CORE, 1]
    half = TILE // 2
    copies = []
    for d, (ref, who) in enumerate(((mine, core), (other, 1 - core))):
        for t in range(8):
            copies.append(
                pltpu.make_async_copy(
                    total.at[8 * d + t], ref.at[pl.ds(TILE * t, TILE)], sems.at[9 * d + t]
                )
            )
        copies.append(
            pltpu.make_async_copy(
                gram.at[pl.ds(pl.multiple_of(who * half, half), half)],
                ref.at[pl.ds(8 * TILE, half)],
                sems.at[9 * d + 8],
            )
        )
    run_all(copies)


def forward_kernel(
    places, residual, b0, b1, b2, b3, b4, b5, b6, b7,
    own_gram, o0, o1, o2, o3, basis, total, gram, cut, sems,
):
    blocks = (b0, b1, b2, b3, b4, b5, b6, b7)
    for d, ref in enumerate(blocks):
        basis[2 * d : 2 * d + 2] = ref[...]
    add_products(1, places, COLS_IN, ROWS_OUT, residual, basis, total)
    copies = []
    gram[...] = gram_of_blocks(blocks)
    half = TILE // 2
    mine = gram[pl.ds(pl.multiple_of(places[COUNT_CORE, 1] * half, half), half)]
    own_gram[...] = mine
    high = mine.astype(BF16)
    low = (mine - high.astype(F32)).astype(BF16)
    for d, ref in enumerate((o1, o2, o3)):
        for t in range(8):
            cut[d, TILE * t : TILE * (t + 1)] = total[8 + 8 * d + t].astype(BF16)
        cut[d, 8 * TILE : 8 * TILE + half] = high
        cut[d, 8 * TILE + half :] = low
        copies.append(pltpu.make_async_copy(cut.at[d], ref, sems.at[d]))
        copies[-1].start()
    o0[...] = total[:8]
    for copy in copies:
        copy.wait()


def inverse_factor_kernel(gram, out):
    size = gram.shape[0]
    panels = size // 8
    wide = (8, size)
    sub = lax.broadcasted_iota(jnp.int32, wide, 0)
    lane = lax.broadcasted_iota(jnp.int32, wide, 1)
    left = [gram[8 * k : 8 * k + 8, :] for k in range(panels)]
    on_diagonal = [lane == sub + 8 * k for k in range(panels)]
    diagonal = sum(jnp.where(on_diagonal[k], left[k], 0.0) for k in range(panels))
    column_scale = 1.0 / jnp.sqrt(jnp.sum(diagonal, axis=0, keepdims=True))
    for k in range(panels):
        row_scale = jnp.sum(jnp.where(on_diagonal[k], column_scale, 0.0), axis=1, keepdims=True)
        left[k] = left[k] * row_scale * column_scale
    right = [jnp.where(on_diagonal[k], 1.0, 0.0).astype(F32) for k in range(panels)]
    for k in range(panels):
        columns = {
            m: [jnp.broadcast_to(left[m][:, 8 * k + j : 8 * k + j + 1], wide) for j in range(8)]
            for m in range(k, panels)
        }
        for i in (0, 2, 4, 6):
            top = columns[k][i][i : i + 1]
            side = columns[k][i + 1][i : i + 1]
            low = columns[k][i + 1][i + 1 : i + 2]
            scale = 1.0 / (top * low - side * side)

            def solve(panel):
                first, second = panel[i : i + 1], panel[i + 1 : i + 2]
                return (low * first - side * second) * scale, (top * second - side * first) * scale

            left_rows, right_rows = solve(left[k]), solve(right[k])
            column_rows = {j: solve(columns[k][j]) for j in range(i + 2, 8)}
            for m in range(k, panels):
                if m == k and i == 6:
                    continue
                c0, c1 = columns[m][i], columns[m][i + 1]
                if m == k:
                    c0, c1 = jnp.where(sub > i + 1, c0, 0.0), jnp.where(sub > i + 1, c1, 0.0)
                left[m] = left[m] - (c0 * left_rows[0] + c1 * left_rows[1])
                right[m] = right[m] - (c0 * right_rows[0] + c1 * right_rows[1])
                for j in range(i + 2, 8):
                    rows = column_rows[j]
                    columns[m][j] = columns[m][j] - (c0 * rows[0] + c1 * rows[1])
    odd = sub % 2 == 1
    for k in range(panels):
        pivot = jnp.sum(jnp.where(on_diagonal[k], left[k], 0.0), axis=1, keepdims=True)
        beside = jnp.where(odd & (lane == sub + 8 * k - 1), left[k], 0.0)
        pivot = jnp.broadcast_to(pivot, wide)
        beside = jnp.broadcast_to(jnp.sum(beside, axis=1, keepdims=True), wide)
        factor = jnp.where(odd, beside / pltpu.roll(pivot, 1, 0), 0.0)
        rows = right[k] - factor * pltpu.roll(right[k], 1, 0)
        out[8 * k : 8 * k + 8, :] = rows * (1.0 / jnp.sqrt(pivot - factor * beside)) * column_scale


def call(kernel, outs, name, flops, ins, arrays, scratch, limit=40, aliases={}):
    return pl.pallas_call(
        kernel,
        out_shape=[jax.ShapeDtypeStruct(shape, dtype) for shape, dtype, _ in outs],
        in_specs=ins,
        out_specs=[place for _, _, place in outs],
        scratch_shapes=scratch,
        input_output_aliases=aliases,
        name=name,
        cost_estimate=pl.CostEstimate(
            flops=flops,
            bytes_accessed=sum(a.size * a.dtype.itemsize for a in arrays),
            transcendentals=0,
        ),
        compiler_params=pltpu.CompilerParams(vmem_limit_bytes=limit * 1024 * 1024),
    )(*arrays)


def gram_of(block):
    return jnp.dot(
        block.T, block, precision=lax.Precision.HIGHEST, preferred_element_type=jnp.float32
    )


def times_inverse(block, inverse):
    return jnp.dot(
        block, inverse.T, precision=lax.Precision.HIGH, preferred_element_type=jnp.float32
    )


def split(value):
    high = value.astype(BF16)
    return high, (value - high.astype(F32)).astype(BF16)


def inverse_factor(gram):
    return call(
        inverse_factor_kernel, [((TILE, TILE), F32, VMEM)], "factor", 4 * TILE**3, [VMEM], (gram,), []
    )[0]


def both_halves(half):
    core = lax.axis_index("core")
    back = hop(half, "core", 1)
    return jnp.concatenate([jnp.where(core == 0, half, back), jnp.where(core == 0, back, half)])


def own_half(gram, core):
    half = gram.shape[0] // 2
    return lax.dynamic_slice_in_dim(gram, core * half, half, 0)


def shards(user_factors, item_factors, start_vectors, ratings, tile_rows, tile_cols, tile_count):
    slots = ratings.shape[2]
    rank = user_factors.shape[1]
    y, core = lax.axis_index("y"), lax.axis_index("core")
    x = lax.axis_index("x")
    rows, cols = tile_rows[0, 0], tile_cols[0, 0]
    work = slots * TILE * TILE
    row_z, row_x = rows // 4, rows % 4
    col_y, col_core, col_i = cols // 4, (cols // 2) % 2, cols % 2
    col_turn = ((core - col_core) % 2) * 8 + col_i
    slot = jnp.arange(slots, dtype=jnp.int32)
    places = jnp.stack(
        [
            jnp.where(slot == 0, tile_count[0, 0], core),
            ((x - row_x) % 4) * 8 + row_z,
            col_turn + ((y - col_y) % 4) * 2,
            ((row_x - x) % 4) * 8 + row_z,
            col_turn + ((col_y - y) % 4) * 2,
            ((y - col_y) % 4) * 4 + ((core - col_core) % 2) * 2 + col_i,
        ]
    )

    factors = jnp.transpose(item_factors.reshape(2, TILE, rank), (0, 2, 1))
    item_share = jnp.concatenate([factors, start_vectors.reshape(2, TILE, TILE)], axis=1)
    items = jnp.concatenate([item_share, hop(item_share, "core", 1)])
    items = gather_axis(items, "y")
    users = gather_axis(gather_z(user_factors.T), "x")
    own_sums = ((8, TILE, TILE), F32, VMEM)
    item_sums = [((8 * TILE + TILE // 2, TILE), F32, HBM)] * 2
    (rated,) = call(
        fetch_kernel, [((slots, TILE, TILE), BF16, VMEM)], "fetch", 0, [HBM], (ratings[0, 0],),
        [pltpu.SemaphoreType.DMA((CHUNKS,))],
    )
    residual, *partial = call(
        first_kernel, [((slots, TILE, TILE), BF16, VMEM), own_sums] + [((8, TILE, TILE), BF16, HBM)] * 3, "first",
        2 * work * (rank + TILE), [SMEM] + [VMEM] * 8 + [VMEM], (places, *users, *items, rated),
        [
            pltpu.VMEM((32, rank, TILE), BF16),
            pltpu.VMEM((16, rank + TILE, TILE), BF16),
            pltpu.VMEM((32, TILE, TILE), F32),
            pltpu.VMEM((24, TILE, TILE), BF16),
            pltpu.SemaphoreType.DMA((8,)),
        ],
        FIRST_LIMIT,
        {9: 0},
    )
    for step in range(2):
        parts = [hop(partial[d], "x", d) for d in range(1, 4)]
        message = partial[0]
        for part in parts:
            tiles = part.reshape(-1, TILE)[: 8 * TILE].reshape(8, TILE, TILE)
            message = message + tiles.astype(F32)
        message = message.astype(Z_TYPE)
        if step == 1:
            half = own_gram
            for part in parts:
                half = half + part[8 * TILE : -(TILE // 2)].astype(F32)
                half = half + part[-(TILE // 2) :].astype(F32)
            high, low = split(half)
            below = jnp.concatenate([high, low]) if Z_TYPE == BF16 else half
            below = jnp.broadcast_to(below[None], (8,) + below.shape)
            message = jnp.concatenate([message, below], axis=1)
        summed = lax.all_to_all(message, "z", 0, 0, tiled=True).astype(F32).sum(axis=0)
        user_share = summed[:TILE]
        if step == 1:
            half = summed[TILE : TILE + TILE // 2]
            if Z_TYPE == BF16:
                half = half + summed[-(TILE // 2) :]
            user_share = times_inverse(user_share, inverse_factor(both_halves(half)))
        user_blocks = gather_axis(gather_z(user_share.astype(BF16)), "x")
        mine, other = call(
            backward_kernel, item_sums, "backward", 4 * work * TILE,
            [SMEM] + [VMEM] * 5, (places, residual, *user_blocks),
            [
                pltpu.VMEM((32, TILE, TILE), BF16),
                pltpu.VMEM((16, TILE, TILE), F32),
                pltpu.VMEM((TILE, TILE), F32),
                pltpu.SemaphoreType.DMA((18,)),
            ],
        )
        mine = mine + hop(other, "core", 1)
        rows_of = 2 * TILE
        high, low = split(mine[4 * rows_of :])
        parts = [
            hop(
                jnp.concatenate([mine[rows_of * d : rows_of * (d + 1)].astype(BF16), high, low]),
                "y", d,
            )
            for d in range(1, 4)
        ]
        share, half = mine[:rows_of], mine[4 * rows_of :]
        for part in parts:
            share = share + part[:rows_of].astype(F32)
            half = half + (
                part[rows_of : -(TILE // 2)].astype(F32) + part[-(TILE // 2) :].astype(F32)
            )
        inverse = inverse_factor(both_halves(half))
        item_share = times_inverse(share, inverse)
        if step == 0:
            blocks = gather_axis(item_share.reshape(2, TILE, TILE).astype(BF16), "y")
            blocks = blocks + [hop(block, "core", 1) for block in blocks]
            own_gram, *partial = call(
                forward_kernel,
                [((TILE // 2, TILE), F32, VMEM), own_sums] + [((9 * TILE, TILE), BF16, HBM)] * 3,
                "forward", 4 * work * TILE, [SMEM] + [VMEM] * 9, (places, residual, *blocks),
                [
                    pltpu.VMEM((16, TILE, TILE), BF16),
                    pltpu.VMEM((32, TILE, TILE), F32),
                    pltpu.VMEM((TILE, TILE), F32),
                    pltpu.VMEM((3, 9 * TILE, TILE), BF16),
                    pltpu.SemaphoreType.DMA((3,)),
                ],
            )
    gram = gram_of(item_share)
    half = own_half(gram, core) + hop(own_half(gram, 1 - core), "core", 1)
    users_total = user_factors.shape[0] * 256
    user_out = times_inverse(user_share, inverse) * jnp.sqrt(F32(users_total))
    half, user_out = lax.optimization_barrier((sum_axis(half, "y"), user_out))
    half = gather_z(sum_axis(half, "x")).sum(axis=0)
    item_inverse = inverse_factor(both_halves(half))
    items_total = item_factors.shape[0] * 256
    item_out = times_inverse(item_share, item_inverse) * jnp.sqrt(F32(items_total))
    return user_out, item_out


def solution(mesh):
    fine = Mesh(mesh.devices.reshape(4, 2, 8, 4), ("y", "core", "z", "x"))
    row, col = ("y", "core"), ("z", "x")
    in_specs = (
        P(row + col, None),
        P(col + row, None),
        P(col + row, None),
        P(row, col, None, None, None),
        P(row, col, None),
        P(row, col, None),
        P(row, col),
    )
    out_specs = (P(row + col, None), P(col + row, None))
    return jax.shard_map(shards, mesh=fine, in_specs=in_specs, out_specs=out_specs, check_vma=False)
```

```python
import jax
import jax.numpy as jnp
from jax import lax
from jax.experimental import pallas as pl
from jax.experimental.pallas import tpu as pltpu
from jax.sharding import Mesh, PartitionSpec as P

F32 = jnp.float32
BF16 = jnp.bfloat16
TILE = 128
GROUP = 48
Z_TYPE = BF16
FIRST_LIMIT = 40
SIZES = {"y": 4, "core": 2, "z": 8, "x": 4}
VMEM = pl.BlockSpec(memory_space=pltpu.VMEM)
SMEM = pl.BlockSpec(memory_space=pltpu.SMEM)
HBM = pl.BlockSpec(memory_space=pltpu.HBM)


def hop(value, axis, distance):
    size = SIZES[axis]
    return lax.ppermute(value, axis, [(i, (i + distance) % size) for i in range(size)])


def far_first(size):
    return sorted(range(1, size), key=lambda d: -min(d, size - d))


def gather_axis(value, axis):
    parts = {d: hop(value, axis, d) for d in far_first(SIZES[axis])}
    return [value] + [parts[d] for d in range(1, SIZES[axis])]


def sum_axis(value, axis):
    total = value
    for part in [hop(value, axis, d) for d in far_first(SIZES[axis])]:
        total = total + part
    return total


def gather_z(value):
    wide = jnp.broadcast_to(value[None], (SIZES["z"],) + value.shape)
    return lax.all_to_all(wide, "z", 0, 0, tiled=True)


CHUNKS = 6
COUNT_CORE, ROWS_IN, COLS_IN, ROWS_OUT, COLS_OUT, START_IN = range(6)


def slot_groups(first, last, body):
    @pl.loop(first, last)
    def _(g):
        body([g * GROUP + u for u in range(GROUP)])


def run_all(copies):
    for copy in copies:
        copy.start()
    for copy in copies:
        copy.wait()


def fetch_kernel(source, out, sems):
    chunk = out.shape[0] // CHUNKS
    places = [pl.ds(c * chunk, chunk) for c in range(CHUNKS)]
    run_all(
        [
            pltpu.make_async_copy(source.at[place], out.at[place], sems.at[c])
            for c, place in enumerate(places)
        ]
    )


def first_kernel(
    places, u0, u1, u2, u3, s0, s1, s2, s3, ratings,
    residual, o0, o1, o2, o3, users, items, total, cut, sems,
):
    count = places[COUNT_CORE, 0]
    for d, ref in enumerate((u0, u1, u2, u3)):
        users[8 * d : 8 * d + 8] = ref[...]
    for d, ref in enumerate((s0, s1, s2, s3)):
        items[4 * d : 4 * d + 4] = ref[...]
    total[...] = jnp.zeros_like(total)
    rank = users.shape[1]

    def body(slots):
        tiles = []
        for k in slots:
            product = lax.dot_general(
                users[places[ROWS_IN, k]],
                items[places[START_IN, k], :rank],
                (((0,), (0,)), ((), ())),
                preferred_element_type=F32,
            )
            value = jnp.where(k < count, product - ratings[k].astype(F32), 0.0)
            tiles.append(value.astype(BF16))
        for k, tile in zip(slots, tiles):
            residual[k] = tile
        parts = [
            jnp.dot(tile, items[places[START_IN, k], rank:], preferred_element_type=F32)
            for k, tile in zip(slots, tiles)
        ]
        for k, part in zip(slots, parts):
            total[places[ROWS_OUT, k]] += part

    slot_groups(0, (count + GROUP - 1) // GROUP, body)
    copies = []
    for d, ref in enumerate((o1, o2, o3)):
        cut[8 * d : 8 * d + 8] = total[8 * d + 8 : 8 * d + 16].astype(BF16)
        copies.append(pltpu.make_async_copy(cut.at[pl.ds(8 * d, 8)], ref, sems.at[d]))
        copies[-1].start()
    o0[...] = total[:8]
    for copy in copies:
        copy.wait()


def gram_of_blocks(blocks):
    total = jnp.zeros((TILE, TILE), F32)
    for block in blocks:

        def step(t, total):
            tiles = block[pl.ds(2 * t, 2)].reshape(2 * TILE, TILE)
            return total + lax.dot_general(
                tiles, tiles, (((0,), (0,)), ((), ())), preferred_element_type=F32
            )

        total = lax.fori_loop(0, block.shape[0] // 2, step, total, unroll=True)
    return total


def add_products(axis, places, from_row, to_row, residual, basis, total):
    total[...] = jnp.zeros_like(total)

    def body(slots):
        parts = []
        for k in slots:
            parts.append(
                lax.dot_general(
                    residual[k], basis[places[from_row, k]], (((axis,), (0,)), ((), ())),
                    preferred_element_type=F32,
                )
            )
        for k, part in zip(slots, parts):
            total[places[to_row, k]] += part

    slot_groups(0, (places[COUNT_CORE, 0] + GROUP - 1) // GROUP, body)


def backward_kernel(places, residual, b0, b1, b2, b3, mine, other, basis, total, gram, sems):
    blocks = (b0, b1, b2, b3)
    for d, ref in enumerate(blocks):
        basis[8 * d : 8 * d + 8] = ref[...]
    add_products(0, places, ROWS_IN, COLS_OUT, residual, basis, total)
    gram[...] = gram_of_blocks(blocks)
    core = places[COUNT_CORE, 1]
    half = TILE // 2
    copies = []
    for d, (ref, who) in enumerate(((mine, core), (other, 1 - core))):
        for t in range(8):
            copies.append(
                pltpu.make_async_copy(
                    total.at[8 * d + t], ref.at[pl.ds(TILE * t, TILE)], sems.at[9 * d + t]
                )
            )
        copies.append(
            pltpu.make_async_copy(
                gram.at[pl.ds(pl.multiple_of(who * half, half), half)],
                ref.at[pl.ds(8 * TILE, half)],
                sems.at[9 * d + 8],
            )
        )
    run_all(copies)


def forward_kernel(
    places, residual, b0, b1, b2, b3, b4, b5, b6, b7,
    own_gram, o0, o1, o2, o3, basis, total, gram, cut, sems,
):
    blocks = (b0, b1, b2, b3, b4, b5, b6, b7)
    for d, ref in enumerate(blocks):
        basis[2 * d : 2 * d + 2] = ref[...]
    add_products(1, places, COLS_IN, ROWS_OUT, residual, basis, total)
    copies = []
    gram[...] = gram_of_blocks(blocks)
    half = TILE // 2
    mine = gram[pl.ds(pl.multiple_of(places[COUNT_CORE, 1] * half, half), half)]
    own_gram[...] = mine
    high = mine.astype(BF16)
    low = (mine - high.astype(F32)).astype(BF16)
    for d, ref in enumerate((o1, o2, o3)):
        for t in range(8):
            cut[d, TILE * t : TILE * (t + 1)] = total[8 + 8 * d + t].astype(BF16)
        cut[d, 8 * TILE : 8 * TILE + half] = high
        cut[d, 8 * TILE + half :] = low
        copies.append(pltpu.make_async_copy(cut.at[d], ref, sems.at[d]))
        copies[-1].start()
    o0[...] = total[:8]
    for copy in copies:
        copy.wait()


def inverse_factor_kernel(gram, out):
    size = gram.shape[0]
    panels = size // 8
    wide = (8, size)
    sub = lax.broadcasted_iota(jnp.int32, wide, 0)
    lane = lax.broadcasted_iota(jnp.int32, wide, 1)
    left = [gram[8 * k : 8 * k + 8, :] for k in range(panels)]
    on_diagonal = [lane == sub + 8 * k for k in range(panels)]
    diagonal = sum(jnp.where(on_diagonal[k], left[k], 0.0) for k in range(panels))
    column_scale = 1.0 / jnp.sqrt(jnp.sum(diagonal, axis=0, keepdims=True))
    for k in range(panels):
        row_scale = jnp.sum(jnp.where(on_diagonal[k], column_scale, 0.0), axis=1, keepdims=True)
        left[k] = left[k] * row_scale * column_scale
    right = [jnp.where(on_diagonal[k], 1.0, 0.0).astype(F32) for k in range(panels)]
    for k in range(panels):
        columns = {
            m: [jnp.broadcast_to(left[m][:, 8 * k + j : 8 * k + j + 1], wide) for j in range(8)]
            for m in range(k, panels)
        }
        for i in (0, 2, 4, 6):
            top = columns[k][i][i : i + 1]
            side = columns[k][i + 1][i : i + 1]
            low = columns[k][i + 1][i + 1 : i + 2]
            scale = 1.0 / (top * low - side * side)

            def solve(panel):
                first, second = panel[i : i + 1], panel[i + 1 : i + 2]
                return (low * first - side * second) * scale, (top * second - side * first) * scale

            left_rows, right_rows = solve(left[k]), solve(right[k])
            column_rows = {j: solve(columns[k][j]) for j in range(i + 2, 8)}
            for m in range(k, panels):
                if m == k and i == 6:
                    continue
                c0, c1 = columns[m][i], columns[m][i + 1]
                if m == k:
                    c0, c1 = jnp.where(sub > i + 1, c0, 0.0), jnp.where(sub > i + 1, c1, 0.0)
                left[m] = left[m] - (c0 * left_rows[0] + c1 * left_rows[1])
                right[m] = right[m] - (c0 * right_rows[0] + c1 * right_rows[1])
                for j in range(i + 2, 8):
                    rows = column_rows[j]
                    columns[m][j] = columns[m][j] - (c0 * rows[0] + c1 * rows[1])
    odd = sub % 2 == 1
    for k in range(panels):
        pivot = jnp.sum(jnp.where(on_diagonal[k], left[k], 0.0), axis=1, keepdims=True)
        beside = jnp.where(odd & (lane == sub + 8 * k - 1), left[k], 0.0)
        pivot = jnp.broadcast_to(pivot, wide)
        beside = jnp.broadcast_to(jnp.sum(beside, axis=1, keepdims=True), wide)
        factor = jnp.where(odd, beside / pltpu.roll(pivot, 1, 0), 0.0)
        rows = right[k] - factor * pltpu.roll(right[k], 1, 0)
        out[8 * k : 8 * k + 8, :] = rows * (1.0 / jnp.sqrt(pivot - factor * beside)) * column_scale


def call(kernel, outs, name, flops, ins, arrays, scratch, limit=40, aliases={}):
    return pl.pallas_call(
        kernel,
        out_shape=[jax.ShapeDtypeStruct(shape, dtype) for shape, dtype, _ in outs],
        in_specs=ins,
        out_specs=[place for _, _, place in outs],
        scratch_shapes=scratch,
        input_output_aliases=aliases,
        name=name,
        cost_estimate=pl.CostEstimate(
            flops=flops,
            bytes_accessed=sum(a.size * a.dtype.itemsize for a in arrays),
            transcendentals=0,
        ),
        compiler_params=pltpu.CompilerParams(vmem_limit_bytes=limit * 1024 * 1024),
    )(*arrays)


def gram_of(block):
    return jnp.dot(
        block.T, block, precision=lax.Precision.HIGHEST, preferred_element_type=jnp.float32
    )


def times_inverse(block, inverse):
    return jnp.dot(
        block, inverse.T, precision=lax.Precision.HIGH, preferred_element_type=jnp.float32
    )


def split(value):
    high = value.astype(BF16)
    return high, (value - high.astype(F32)).astype(BF16)


def inverse_factor(gram):
    return call(
        inverse_factor_kernel, [((TILE, TILE), F32, VMEM)], "factor", 4 * TILE**3, [VMEM], (gram,), []
    )[0]


def both_halves(half):
    core = lax.axis_index("core")
    back = hop(half, "core", 1)
    return jnp.concatenate([jnp.where(core == 0, half, back), jnp.where(core == 0, back, half)])


def own_half(gram, core):
    half = gram.shape[0] // 2
    return lax.dynamic_slice_in_dim(gram, core * half, half, 0)


def shards(user_factors, item_factors, start_vectors, ratings, tile_rows, tile_cols, tile_count):
    slots = ratings.shape[2]
    rank = user_factors.shape[1]
    y, core = lax.axis_index("y"), lax.axis_index("core")
    x = lax.axis_index("x")
    rows, cols = tile_rows[0, 0], tile_cols[0, 0]
    work = slots * TILE * TILE
    row_z, row_x = rows // 4, rows % 4
    col_y, col_core, col_i = cols // 4, (cols // 2) % 2, cols % 2
    col_turn = ((core - col_core) % 2) * 8 + col_i
    slot = jnp.arange(slots, dtype=jnp.int32)
    places = jnp.stack(
        [
            jnp.where(slot == 0, tile_count[0, 0], core),
            ((x - row_x) % 4) * 8 + row_z,
            col_turn + ((y - col_y) % 4) * 2,
            ((row_x - x) % 4) * 8 + row_z,
            col_turn + ((col_y - y) % 4) * 2,
            ((y - col_y) % 4) * 4 + ((core - col_core) % 2) * 2 + col_i,
        ]
    )

    factors = jnp.transpose(item_factors.reshape(2, TILE, rank), (0, 2, 1))
    item_share = jnp.concatenate([factors, start_vectors.reshape(2, TILE, TILE)], axis=1)
    items = jnp.concatenate([item_share, hop(item_share, "core", 1)])
    items = gather_axis(items, "y")
    users = gather_axis(gather_z(user_factors.T), "x")
    own_sums = ((8, TILE, TILE), F32, VMEM)
    item_sums = [((8 * TILE + TILE // 2, TILE), F32, HBM)] * 2
    items[1], listed = lax.optimization_barrier((items[1], ratings[0, 0]))
    (rated,) = call(
        fetch_kernel, [((slots, TILE, TILE), BF16, VMEM)], "fetch", 0, [HBM], (listed,),
        [pltpu.SemaphoreType.DMA((CHUNKS,))],
    )
    residual, *partial = call(
        first_kernel, [((slots, TILE, TILE), BF16, VMEM), own_sums] + [((8, TILE, TILE), BF16, HBM)] * 3, "first",
        2 * work * (rank + TILE), [SMEM] + [VMEM] * 8 + [VMEM], (places, *users, *items, rated),
        [
            pltpu.VMEM((32, rank, TILE), BF16),
            pltpu.VMEM((16, rank + TILE, TILE), BF16),
            pltpu.VMEM((32, TILE, TILE), F32),
            pltpu.VMEM((24, TILE, TILE), BF16),
            pltpu.SemaphoreType.DMA((8,)),
        ],
        FIRST_LIMIT,
        {9: 0},
    )
    for step in range(2):
        parts = [hop(partial[d], "x", d) for d in far_first(4)]
        message = partial[0]
        for part in parts:
            tiles = part.reshape(-1, TILE)[: 8 * TILE].reshape(8, TILE, TILE)
            message = message + tiles.astype(F32)
        message = message.astype(Z_TYPE)
        if step == 1:
            half = own_gram
            for part in parts:
                half = half + part[8 * TILE : -(TILE // 2)].astype(F32)
                half = half + part[-(TILE // 2) :].astype(F32)
            high, low = split(half)
            below = jnp.concatenate([high, low]) if Z_TYPE == BF16 else half
            below = jnp.broadcast_to(below[None], (8,) + below.shape)
            message = jnp.concatenate([message, below], axis=1)
        summed = lax.all_to_all(message, "z", 0, 0, tiled=True).astype(F32).sum(axis=0)
        user_share = summed[:TILE]
        if step == 1:
            half = summed[TILE : TILE + TILE // 2]
            if Z_TYPE == BF16:
                half = half + summed[-(TILE // 2) :]
            user_share = times_inverse(user_share, inverse_factor(both_halves(half)))
        user_blocks = gather_axis(gather_z(user_share.astype(BF16)), "x")
        mine, other = call(
            backward_kernel, item_sums, "backward", 4 * work * TILE,
            [SMEM] + [VMEM] * 5, (places, residual, *user_blocks),
            [
                pltpu.VMEM((32, TILE, TILE), BF16),
                pltpu.VMEM((16, TILE, TILE), F32),
                pltpu.VMEM((TILE, TILE), F32),
                pltpu.SemaphoreType.DMA((18,)),
            ],
        )
        mine = mine + hop(other, "core", 1)
        rows_of = 2 * TILE
        high, low = split(mine[4 * rows_of :])
        parts = [
            hop(
                jnp.concatenate([mine[rows_of * d : rows_of * (d + 1)].astype(BF16), high, low]),
                "y", d,
            )
            for d in far_first(4)
        ]
        share, half = mine[:rows_of], mine[4 * rows_of :]
        for part in parts:
            share = share + part[:rows_of].astype(F32)
            half = half + (
                part[rows_of : -(TILE // 2)].astype(F32) + part[-(TILE // 2) :].astype(F32)
            )
        inverse = inverse_factor(both_halves(half))
        item_share = times_inverse(share, inverse)
        if step == 0:
            blocks = gather_axis(item_share.reshape(2, TILE, TILE).astype(BF16), "y")
            blocks = blocks + [hop(block, "core", 1) for block in blocks]
            own_gram, *partial = call(
                forward_kernel,
                [((TILE // 2, TILE), F32, VMEM), own_sums] + [((9 * TILE, TILE), BF16, HBM)] * 3,
                "forward", 4 * work * TILE, [SMEM] + [VMEM] * 9, (places, residual, *blocks),
                [
                    pltpu.VMEM((16, TILE, TILE), BF16),
                    pltpu.VMEM((32, TILE, TILE), F32),
                    pltpu.VMEM((TILE, TILE), F32),
                    pltpu.VMEM((3, 9 * TILE, TILE), BF16),
                    pltpu.SemaphoreType.DMA((3,)),
                ],
            )
    gram = gram_of(item_share)
    half = own_half(gram, core) + hop(own_half(gram, 1 - core), "core", 1)
    users_total = user_factors.shape[0] * 256
    user_out = times_inverse(user_share, inverse) * jnp.sqrt(F32(users_total))
    half, user_out = lax.optimization_barrier((sum_axis(half, "y"), user_out))
    half = gather_z(sum_axis(half, "x")).sum(axis=0)
    item_inverse = inverse_factor(both_halves(half))
    items_total = item_factors.shape[0] * 256
    item_out = times_inverse(item_share, item_inverse) * jnp.sqrt(F32(items_total))
    return user_out, item_out


def solution(mesh):
    fine = Mesh(mesh.devices.reshape(4, 2, 8, 4), ("y", "core", "z", "x"))
    row, col = ("y", "core"), ("z", "x")
    in_specs = (
        P(row + col, None),
        P(col + row, None),
        P(col + row, None),
        P(row, col, None, None, None),
        P(row, col, None),
        P(row, col, None),
        P(row, col),
    )
    out_specs = (P(row + col, None), P(col + row, None))
    return jax.shard_map(shards, mesh=fine, in_specs=in_specs, out_specs=out_specs, check_vma=False)
```

```python
import jax
import jax.numpy as jnp
from jax import lax
from jax.experimental import pallas as pl
from jax.experimental.pallas import tpu as pltpu
from jax.sharding import Mesh, PartitionSpec as P

F32 = jnp.float32
BF16 = jnp.bfloat16
TILE = 128
GROUP = 48
Z_TYPE = BF16
FIRST_LIMIT = 40
SIZES = {"y": 4, "core": 2, "z": 8, "x": 4}
VMEM = pl.BlockSpec(memory_space=pltpu.VMEM)
SMEM = pl.BlockSpec(memory_space=pltpu.SMEM)
HBM = pl.BlockSpec(memory_space=pltpu.HBM)


def hop(value, axis, distance):
    size = SIZES[axis]
    return lax.ppermute(value, axis, [(i, (i + distance) % size) for i in range(size)])


def far_first(size):
    return sorted(range(1, size), key=lambda d: -min(d, size - d))


def gather_axis(value, axis):
    parts = {d: hop(value, axis, d) for d in far_first(SIZES[axis])}
    return [value] + [parts[d] for d in range(1, SIZES[axis])]


def sum_axis(value, axis):
    total = value
    for part in [hop(value, axis, d) for d in far_first(SIZES[axis])]:
        total = total + part
    return total


def gather_z(value):
    wide = jnp.broadcast_to(value[None], (SIZES["z"],) + value.shape)
    return lax.all_to_all(wide, "z", 0, 0, tiled=True)


CHUNKS = 6
COUNT_CORE, ROWS_IN, COLS_IN, ROWS_OUT, COLS_OUT, START_IN = range(6)


def slot_groups(first, last, body):
    @pl.loop(first, last)
    def _(g):
        body([g * GROUP + u for u in range(GROUP)])


def run_all(copies):
    for copy in copies:
        copy.start()
    for copy in copies:
        copy.wait()


def fetch_kernel(source, out, sems):
    chunk = out.shape[0] // CHUNKS
    places = [pl.ds(c * chunk, chunk) for c in range(CHUNKS)]
    run_all(
        [
            pltpu.make_async_copy(source.at[place], out.at[place], sems.at[c])
            for c, place in enumerate(places)
        ]
    )


def first_kernel(
    places, u0, u1, u2, u3, s0, s1, s2, s3, ratings,
    residual, o0, o1, o2, o3, users, items, total, cut, sems,
):
    count = places[COUNT_CORE, 0]
    for d, ref in enumerate((u0, u1, u2, u3)):
        users[8 * d : 8 * d + 8] = ref[...]
    for d, ref in enumerate((s0, s1, s2, s3)):
        items[4 * d : 4 * d + 4] = ref[...]
    total[...] = jnp.zeros_like(total)
    rank = users.shape[1]

    def body(slots):
        tiles = []
        for k in slots:
            product = lax.dot_general(
                users[places[ROWS_IN, k]],
                items[places[START_IN, k], :rank],
                (((0,), (0,)), ((), ())),
                preferred_element_type=F32,
            )
            value = jnp.where(k < count, product - ratings[k].astype(F32), 0.0)
            tiles.append(value.astype(BF16))
        for k, tile in zip(slots, tiles):
            residual[k] = tile
        parts = [
            jnp.dot(tile, items[places[START_IN, k], rank:], preferred_element_type=F32)
            for k, tile in zip(slots, tiles)
        ]
        for k, part in zip(slots, parts):
            total[places[ROWS_OUT, k]] += part

    slot_groups(0, (count + GROUP - 1) // GROUP, body)
    copies = []
    for d, ref in enumerate((o1, o2, o3)):
        cut[8 * d : 8 * d + 8] = total[8 * d + 8 : 8 * d + 16].astype(BF16)
        copies.append(pltpu.make_async_copy(cut.at[pl.ds(8 * d, 8)], ref, sems.at[d]))
        copies[-1].start()
    o0[...] = total[:8]
    for copy in copies:
        copy.wait()


def gram_of_blocks(blocks):
    total = jnp.zeros((TILE, TILE), F32)
    for block in blocks:

        def step(t, total):
            tiles = block[pl.ds(2 * t, 2)].reshape(2 * TILE, TILE)
            return total + lax.dot_general(
                tiles, tiles, (((0,), (0,)), ((), ())), preferred_element_type=F32
            )

        total = lax.fori_loop(0, block.shape[0] // 2, step, total, unroll=True)
    return total


def add_products(axis, places, from_row, to_row, residual, basis, total):
    total[...] = jnp.zeros_like(total)

    def body(slots):
        parts = []
        for k in slots:
            parts.append(
                lax.dot_general(
                    residual[k], basis[places[from_row, k]], (((axis,), (0,)), ((), ())),
                    preferred_element_type=F32,
                )
            )
        for k, part in zip(slots, parts):
            total[places[to_row, k]] += part

    slot_groups(0, (places[COUNT_CORE, 0] + GROUP - 1) // GROUP, body)


def backward_kernel(places, residual, b0, b1, b2, b3, mine, other, basis, total, gram, sems):
    blocks = (b0, b1, b2, b3)
    for d, ref in enumerate(blocks):
        basis[8 * d : 8 * d + 8] = ref[...]
    add_products(0, places, ROWS_IN, COLS_OUT, residual, basis, total)
    core = places[COUNT_CORE, 1]
    half = TILE // 2
    copies = [
        pltpu.make_async_copy(
            total.at[8 * d + t], ref.at[pl.ds(TILE * t, TILE)], sems.at[9 * d + t]
        )
        for d, ref in ((1, other), (0, mine))
        for t in range(8)
    ]
    for copy in copies:
        copy.start()
    gram[...] = gram_of_blocks(blocks)
    for d, ref, who in ((1, other, 1 - core), (0, mine, core)):
        copies.append(
            pltpu.make_async_copy(
                gram.at[pl.ds(pl.multiple_of(who * half, half), half)],
                ref.at[pl.ds(8 * TILE, half)],
                sems.at[9 * d + 8],
            )
        )
        copies[-1].start()
    for copy in copies:
        copy.wait()


def forward_kernel(
    places, residual, b0, b1, b2, b3, b4, b5, b6, b7,
    own_gram, o0, o1, o2, o3, basis, total, gram, cut, sems,
):
    blocks = (b0, b1, b2, b3, b4, b5, b6, b7)
    for d, ref in enumerate(blocks):
        basis[2 * d : 2 * d + 2] = ref[...]
    add_products(1, places, COLS_IN, ROWS_OUT, residual, basis, total)
    copies = []
    gram[...] = gram_of_blocks(blocks)
    half = TILE // 2
    mine = gram[pl.ds(pl.multiple_of(places[COUNT_CORE, 1] * half, half), half)]
    own_gram[...] = mine
    high = mine.astype(BF16)
    low = (mine - high.astype(F32)).astype(BF16)
    for d, ref in enumerate((o1, o2, o3)):
        for t in range(8):
            cut[d, TILE * t : TILE * (t + 1)] = total[8 + 8 * d + t].astype(BF16)
        cut[d, 8 * TILE : 8 * TILE + half] = high
        cut[d, 8 * TILE + half :] = low
        copies.append(pltpu.make_async_copy(cut.at[d], ref, sems.at[d]))
        copies[-1].start()
    o0[...] = total[:8]
    for copy in copies:
        copy.wait()


def inverse_factor_kernel(gram, out):
    size = gram.shape[0]
    panels = size // 8
    wide = (8, size)
    sub = lax.broadcasted_iota(jnp.int32, wide, 0)
    lane = lax.broadcasted_iota(jnp.int32, wide, 1)
    left = [gram[8 * k : 8 * k + 8, :] for k in range(panels)]
    on_diagonal = [lane == sub + 8 * k for k in range(panels)]
    diagonal = sum(jnp.where(on_diagonal[k], left[k], 0.0) for k in range(panels))
    column_scale = 1.0 / jnp.sqrt(jnp.sum(diagonal, axis=0, keepdims=True))
    for k in range(panels):
        row_scale = jnp.sum(jnp.where(on_diagonal[k], column_scale, 0.0), axis=1, keepdims=True)
        left[k] = left[k] * row_scale * column_scale
    right = [jnp.where(on_diagonal[k], 1.0, 0.0).astype(F32) for k in range(panels)]
    for k in range(panels):
        columns = {
            m: [jnp.broadcast_to(left[m][:, 8 * k + j : 8 * k + j + 1], wide) for j in range(8)]
            for m in range(k, panels)
        }
        for i in (0, 2, 4, 6):
            top = columns[k][i][i : i + 1]
            side = columns[k][i + 1][i : i + 1]
            low = columns[k][i + 1][i + 1 : i + 2]
            scale = 1.0 / (top * low - side * side)

            def solve(panel):
                first, second = panel[i : i + 1], panel[i + 1 : i + 2]
                return (low * first - side * second) * scale, (top * second - side * first) * scale

            left_rows, right_rows = solve(left[k]), solve(right[k])
            column_rows = {j: solve(columns[k][j]) for j in range(i + 2, 8)}
            for m in range(k, panels):
                if m == k and i == 6:
                    continue
                c0, c1 = columns[m][i], columns[m][i + 1]
                if m == k:
                    c0, c1 = jnp.where(sub > i + 1, c0, 0.0), jnp.where(sub > i + 1, c1, 0.0)
                left[m] = left[m] - (c0 * left_rows[0] + c1 * left_rows[1])
                right[m] = right[m] - (c0 * right_rows[0] + c1 * right_rows[1])
                for j in range(i + 2, 8):
                    rows = column_rows[j]
                    columns[m][j] = columns[m][j] - (c0 * rows[0] + c1 * rows[1])
    odd = sub % 2 == 1
    for k in range(panels):
        pivot = jnp.sum(jnp.where(on_diagonal[k], left[k], 0.0), axis=1, keepdims=True)
        beside = jnp.where(odd & (lane == sub + 8 * k - 1), left[k], 0.0)
        pivot = jnp.broadcast_to(pivot, wide)
        beside = jnp.broadcast_to(jnp.sum(beside, axis=1, keepdims=True), wide)
        factor = jnp.where(odd, beside / pltpu.roll(pivot, 1, 0), 0.0)
        rows = right[k] - factor * pltpu.roll(right[k], 1, 0)
        out[8 * k : 8 * k + 8, :] = rows * (1.0 / jnp.sqrt(pivot - factor * beside)) * column_scale


def call(kernel, outs, name, flops, ins, arrays, scratch, limit=40, aliases={}):
    return pl.pallas_call(
        kernel,
        out_shape=[jax.ShapeDtypeStruct(shape, dtype) for shape, dtype, _ in outs],
        in_specs=ins,
        out_specs=[place for _, _, place in outs],
        scratch_shapes=scratch,
        input_output_aliases=aliases,
        name=name,
        cost_estimate=pl.CostEstimate(
            flops=flops,
            bytes_accessed=sum(a.size * a.dtype.itemsize for a in arrays),
            transcendentals=0,
        ),
        compiler_params=pltpu.CompilerParams(vmem_limit_bytes=limit * 1024 * 1024),
    )(*arrays)


def gram_of(block):
    return jnp.dot(
        block.T, block, precision=lax.Precision.HIGHEST, preferred_element_type=jnp.float32
    )


def times_inverse(block, inverse):
    return jnp.dot(
        block, inverse.T, precision=lax.Precision.HIGH, preferred_element_type=jnp.float32
    )


def split(value):
    high = value.astype(BF16)
    return high, (value - high.astype(F32)).astype(BF16)


def inverse_factor(gram):
    return call(
        inverse_factor_kernel, [((TILE, TILE), F32, VMEM)], "factor", 4 * TILE**3, [VMEM], (gram,), []
    )[0]


def both_halves(half):
    core = lax.axis_index("core")
    back = hop(half, "core", 1)
    return jnp.concatenate([jnp.where(core == 0, half, back), jnp.where(core == 0, back, half)])


def own_half(gram, core):
    half = gram.shape[0] // 2
    return lax.dynamic_slice_in_dim(gram, core * half, half, 0)


def shards(user_factors, item_factors, start_vectors, ratings, tile_rows, tile_cols, tile_count):
    slots = ratings.shape[2]
    rank = user_factors.shape[1]
    y, core = lax.axis_index("y"), lax.axis_index("core")
    x = lax.axis_index("x")
    rows, cols = tile_rows[0, 0], tile_cols[0, 0]
    work = slots * TILE * TILE
    row_z, row_x = rows // 4, rows % 4
    col_y, col_core, col_i = cols // 4, (cols // 2) % 2, cols % 2
    col_turn = ((core - col_core) % 2) * 8 + col_i
    slot = jnp.arange(slots, dtype=jnp.int32)
    places = jnp.stack(
        [
            jnp.where(slot == 0, tile_count[0, 0], core),
            ((x - row_x) % 4) * 8 + row_z,
            col_turn + ((y - col_y) % 4) * 2,
            ((row_x - x) % 4) * 8 + row_z,
            col_turn + ((col_y - y) % 4) * 2,
            ((y - col_y) % 4) * 4 + ((core - col_core) % 2) * 2 + col_i,
        ]
    )

    factors = jnp.transpose(item_factors.reshape(2, TILE, rank), (0, 2, 1))
    item_share = jnp.concatenate([factors, start_vectors.reshape(2, TILE, TILE)], axis=1)
    items = jnp.concatenate([item_share, hop(item_share, "core", 1)])
    items = gather_axis(items, "y")
    users = gather_axis(gather_z(user_factors.T), "x")
    own_sums = ((8, TILE, TILE), F32, VMEM)
    item_sums = [((8 * TILE + TILE // 2, TILE), F32, HBM)] * 2
    items[1], listed = lax.optimization_barrier((items[1], ratings[0, 0]))
    (rated,) = call(
        fetch_kernel, [((slots, TILE, TILE), BF16, VMEM)], "fetch", 0, [HBM], (listed,),
        [pltpu.SemaphoreType.DMA((CHUNKS,))],
    )
    residual, *partial = call(
        first_kernel, [((slots, TILE, TILE), BF16, VMEM), own_sums] + [((8, TILE, TILE), BF16, HBM)] * 3, "first",
        2 * work * (rank + TILE), [SMEM] + [VMEM] * 8 + [VMEM], (places, *users, *items, rated),
        [
            pltpu.VMEM((32, rank, TILE), BF16),
            pltpu.VMEM((16, rank + TILE, TILE), BF16),
            pltpu.VMEM((32, TILE, TILE), F32),
            pltpu.VMEM((24, TILE, TILE), BF16),
            pltpu.SemaphoreType.DMA((8,)),
        ],
        FIRST_LIMIT,
        {9: 0},
    )
    for step in range(2):
        parts = [hop(partial[d], "x", d) for d in far_first(4)]
        message = partial[0]
        for part in parts:
            tiles = part.reshape(-1, TILE)[: 8 * TILE].reshape(8, TILE, TILE)
            message = message + tiles.astype(F32)
        message = message.astype(Z_TYPE)
        if step == 1:
            half = own_gram
            for part in parts:
                half = half + part[8 * TILE : -(TILE // 2)].astype(F32)
                half = half + part[-(TILE // 2) :].astype(F32)
            high, low = split(half)
            below = jnp.concatenate([high, low]) if Z_TYPE == BF16 else half
            below = jnp.broadcast_to(below[None], (8,) + below.shape)
            message = jnp.concatenate([message, below], axis=1)
        summed = lax.all_to_all(message, "z", 0, 0, tiled=True).astype(F32).sum(axis=0)
        user_share = summed[:TILE]
        if step == 1:
            half = summed[TILE : TILE + TILE // 2]
            if Z_TYPE == BF16:
                half = half + summed[-(TILE // 2) :]
            user_share = times_inverse(user_share, inverse_factor(both_halves(half)))
        user_blocks = gather_axis(gather_z(user_share.astype(BF16)), "x")
        mine, other = call(
            backward_kernel, item_sums, "backward", 4 * work * TILE,
            [SMEM] + [VMEM] * 5, (places, residual, *user_blocks),
            [
                pltpu.VMEM((32, TILE, TILE), BF16),
                pltpu.VMEM((16, TILE, TILE), F32),
                pltpu.VMEM((TILE, TILE), F32),
                pltpu.SemaphoreType.DMA((18,)),
            ],
        )
        mine = mine + hop(other, "core", 1)
        rows_of = 2 * TILE
        high, low = split(mine[4 * rows_of :])
        parts = [
            hop(
                jnp.concatenate([mine[rows_of * d : rows_of * (d + 1)].astype(BF16), high, low]),
                "y", d,
            )
            for d in far_first(4)
        ]
        share, half = mine[:rows_of], mine[4 * rows_of :]
        for part in parts:
            share = share + part[:rows_of].astype(F32)
            half = half + (
                part[rows_of : -(TILE // 2)].astype(F32) + part[-(TILE // 2) :].astype(F32)
            )
        inverse = inverse_factor(both_halves(half))
        item_share = times_inverse(share, inverse)
        if step == 0:
            blocks = gather_axis(item_share.reshape(2, TILE, TILE).astype(BF16), "y")
            blocks = blocks + [hop(block, "core", 1) for block in blocks]
            own_gram, *partial = call(
                forward_kernel,
                [((TILE // 2, TILE), F32, VMEM), own_sums] + [((9 * TILE, TILE), BF16, HBM)] * 3,
                "forward", 4 * work * TILE, [SMEM] + [VMEM] * 9, (places, residual, *blocks),
                [
                    pltpu.VMEM((16, TILE, TILE), BF16),
                    pltpu.VMEM((32, TILE, TILE), F32),
                    pltpu.VMEM((TILE, TILE), F32),
                    pltpu.VMEM((3, 9 * TILE, TILE), BF16),
                    pltpu.SemaphoreType.DMA((3,)),
                ],
            )
    gram = gram_of(item_share)
    half = own_half(gram, core) + hop(own_half(gram, 1 - core), "core", 1)
    users_total = user_factors.shape[0] * 256
    user_out = times_inverse(user_share, inverse) * jnp.sqrt(F32(users_total))
    half, user_out = lax.optimization_barrier((sum_axis(half, "y"), user_out))
    half = gather_z(sum_axis(half, "x")).sum(axis=0)
    item_inverse = inverse_factor(both_halves(half))
    items_total = item_factors.shape[0] * 256
    item_out = times_inverse(item_share, item_inverse) * jnp.sqrt(F32(items_total))
    return user_out, item_out


def solution(mesh):
    fine = Mesh(mesh.devices.reshape(4, 2, 8, 4), ("y", "core", "z", "x"))
    row, col = ("y", "core"), ("z", "x")
    in_specs = (
        P(row + col, None),
        P(col + row, None),
        P(col + row, None),
        P(row, col, None, None, None),
        P(row, col, None),
        P(row, col, None),
        P(row, col),
    )
    out_specs = (P(row + col, None), P(col + row, None))
    return jax.shard_map(shards, mesh=fine, in_specs=in_specs, out_specs=out_specs, check_vma=False)
```
